32 devices in a mesh: dp: 4 (over x, core), row: 2 (over y), col: 4 (over z).
Axes of the slice: x: 2, y: 2, z: 4, core: 2. Of those that a mesh axis runs over, the one named last changes fastest.
Arguments:
- latents: bfloat16 [4096, 768], P(('dp', 'col'), 'row'), may hold values from -6 to 6
- labels: int32 [16], P('dp'), may hold values from 0 to 999
- step_ids: int32 [16], P('dp'), may hold values from 0 to 999
- class_table: bfloat16 [1000, 768], P('col'), may hold values from -6 to 6
- step_table: bfloat16 [1000, 768], P('col'), may hold values from -6 to 6
- w_ada: bfloat16 [1, 768, 6, 768], P(None, 'col', None, 'row'), may hold values from -0.21875 to 0.21875
- b_ada: bfloat16 [1, 6, 768], P(None, None, 'row'), may hold values from -3 to 3
- w_qkv: bfloat16 [1, 768, 3, 768], P(None, 'row', None, 'col'), may hold values from -0.21875 to 0.21875
- b_qkv: bfloat16 [1, 2, 768], P(None, None, 'col'), may hold values from -3 to 3
- w_out: bfloat16 [1, 768, 768], P(None, 'col', 'row'), may hold values from -0.875 to 0.875
- b_out: bfloat16 [1, 768], P(None, 'row'), may hold values from -3 to 3
- w_up: bfloat16 [1, 768, 3072], P(None, 'row', 'col'), may hold values from -0.21875 to 0.21875
- b_up: bfloat16 [1, 3072], P(None, 'col'), may hold values from -3 to 3
- w_down: bfloat16 [1, 3072, 768], P(None, 'col', 'row'), may hold values from -0.109375 to 0.109375
- b_down: bfloat16 [1, 768], P(None, 'row'), may hold values from -3 to 3
- cotangent: bfloat16 [4096, 768], P(('dp', 'col'), 'row'), may hold values from -6 to 6
Outputs:
- output: bfloat16 [4096, 768], P(('dp', 'col'), 'row')
- grad_latents: bfloat16 [4096, 768], P(('dp', 'col'), 'row')
- grad_class_table: float32 [1000, 768], P('col')
- grad_step_table: float32 [1000, 768], P('col')
- grad_w_ada: float32 [1, 768, 6, 768], P(None, 'col', None, 'row')
- grad_b_ada: float32 [1, 6, 768], P(None, None, 'row')
- grad_w_qkv: float32 [1, 768, 3, 768], P(None, 'row', None, 'col')
- grad_b_qkv: float32 [1, 2, 768], P(None, None, 'col')
- grad_w_out: float32 [1, 768, 768], P(None, 'col', 'row')
- grad_b_out: float32 [1, 768], P(None, 'row')
- grad_w_up: float32 [1, 768, 3072], P(None, 'row', 'col')
- grad_b_up: float32 [1, 3072], P(None, 'col')
- grad_w_down: float32 [1, 3072, 768], P(None, 'col', 'row')
- grad_b_down: float32 [1, 768], P(None, 'row')
The draws below stay inside these ranges and needn't reach their ends.
All inputs are finite; a program needn't handle non-finite values.
Results may differ from the reference program's by a relative error of at most 0.015.
The reference program's roundings to bfloat16 on the way count: a program that leaves them out, or rounds other values in their place, can miss the bound.
Values may be sent and summed in bfloat16 or wider, within the bound.
No kernel may reach another device: no remote copies, remote signals or barrier semaphores. Data moves between devices by JAX's collectives and lax.ppermute only.
A program may use at most 192 MiB of HBM per device.

```python
import jax
import jax.numpy as jnp
from jax import lax

D = 768
FF = 3072
CLASSES = 1000
STEPS = 1000
HEAD_DIM = 64
LENGTH = 256
LAYERS = 1
HEADS = 12
BATCH = 16
TOKENS = 4096
N_DP = 4


def with_ends(entries, own_key, least, largest):
    dims = entries.shape
    index_at = [jax.random.randint(jax.random.fold_in(own_key, axis), (), 0, dims[axis]) for axis in range(len(dims))]
    entries = entries.at[tuple(index_at)].set(least)
    longest = dims.index(max(dims))
    index_at[longest] = (index_at[longest] + 1) % dims[longest]
    return entries.at[tuple(index_at)].set(largest)


def block_scale(rng, dims, cuts, least, top_value):
    gain = 1.0
    for position, blocks in cuts:
        draws = jax.random.uniform(jax.random.fold_in(jax.random.fold_in(rng, 6), position), (blocks,), jnp.float32, least / len(cuts), top_value / len(cuts))
        gain = gain * jnp.repeat(jnp.exp(draws), dims[position] // blocks).reshape((-1,) + (1,) * (len(dims) - 1 - position))
    return gain


def centred(rng, extent, spread, bound, split=(), held_as=jnp.bfloat16):
    loudness = block_scale(rng, extent, split, -0.22, 0.18) if split else 1.0
    drawn = jax.random.normal(rng, extent, jnp.float32) * spread * loudness
    return jnp.minimum(jnp.maximum(drawn, -bound), bound).astype(held_as)


def setup_inputs(seed: int = 0) -> dict:
    key_list = jax.random.split(jax.random.key(seed), 17)
    latents = centred(key_list[0], (TOKENS, D), 1.0, 6.0, ((0, 16), (1, 2)))
    labels = with_ends(jax.random.randint(key_list[1], (BATCH,), 0, CLASSES), jax.random.fold_in(key_list[1], 1), 0, CLASSES - 1).astype(jnp.int32)
    step_ids = with_ends(jax.random.randint(key_list[2], (BATCH,), 0, STEPS), jax.random.fold_in(key_list[2], 1), 0, STEPS - 1).astype(jnp.int32)
    class_table = centred(key_list[3], (CLASSES, D), 1.0, 6.0, ((0, 4),))
    step_table = centred(key_list[4], (STEPS, D), 1.0, 6.0, ((0, 4),))
    w_ada = centred(key_list[5], (LAYERS, D, 6, D), D ** -0.5, 0.21875, ((1, 4), (3, 2)))
    b_ada = centred(key_list[6], (LAYERS, 6, D), 0.5, 3.0, ((2, 2),))
    w_qkv = centred(key_list[7], (LAYERS, D, 3, D), D ** -0.5, 0.21875, ((1, 2), (3, 4)))
    b_qkv = centred(key_list[8], (LAYERS, 2, D), 0.5, 3.0, ((2, 4),))
    w_out = centred(key_list[9], (LAYERS, D, D), (D // 16) ** -0.5, 0.875, ((1, 4), (2, 2)))
    b_out = centred(key_list[10], (LAYERS, D), 0.5, 3.0, ((1, 2),))
    w_up = centred(key_list[11], (LAYERS, D, FF), D ** -0.5, 0.21875, ((1, 2), (2, 4)))
    b_up = centred(key_list[12], (LAYERS, FF), 0.5, 3.0, ((1, 4),))
    w_down = centred(key_list[13], (LAYERS, FF, D), FF ** -0.5, 0.109375, ((1, 4), (2, 2)))
    b_down = centred(key_list[14], (LAYERS, D), 0.5, 3.0, ((1, 2),))
    cotangent = centred(key_list[15], (TOKENS, D), 1.0, 6.0, ((0, 16), (1, 2)))
    return dict(latents=latents, labels=labels, step_ids=step_ids, class_table=class_table, step_table=step_table, w_ada=w_ada, b_ada=b_ada, w_qkv=w_qkv, b_qkv=b_qkv, w_out=w_out, b_out=b_out, w_up=w_up, b_up=b_up, w_down=w_down, b_down=b_down, cotangent=cotangent)


PRECISE = lax.Precision.HIGHEST
NORM_EPSILON = 1e-06

@jax.custom_vjp
def low(v):
    return lax.optimization_barrier(v.astype(jnp.bfloat16)).astype(jnp.float32)

@jax.custom_vjp
def low_back(v):
    return v

def low_keep(v):
    return (low(v), None)

def low_pass(kept, grad):
    return (grad,)

def back_keep(v):
    return (v, None)

def back_low(kept, grad):
    return (low(grad),)
low.defvjp(low_keep, low_pass)
low_back.defvjp(back_keep, back_low)

def layer_norm(values):
    center = values - lax.optimization_barrier(jnp.mean(values, axis=-1, keepdims=True))
    variance = lax.optimization_barrier(jnp.mean(center * center, axis=-1, keepdims=True))
    return center * lax.rsqrt(variance + NORM_EPSILON)

def rounded_both(values):
    return low(low_back(values))

def two_blocks(rows_in, modulate, w_qkv, b_qkv, w_out, b_out, w_up, b_up, w_down, b_down):
    head_shape = (-1, LENGTH, HEADS, HEAD_DIM)
    score_scale = HEAD_DIM ** (-0.5)
    residual = rows_in
    for layer_at in range(LAYERS):
        factors = modulate[:, layer_at]
        normed_in = low(layer_norm(residual) * (1.0 + factors[:, 1]) + factors[:, 0])
        projected = jnp.dot(normed_in, w_qkv[layer_at].reshape(D, 3 * D), precision=PRECISE)
        queries = rounded_both(projected[:, :D] + b_qkv[layer_at, 0]).reshape(head_shape)
        key_rows = rounded_both(projected[:, D:2 * D]).reshape(head_shape)
        value_rows = rounded_both(projected[:, 2 * D:] + b_qkv[layer_at, 1]).reshape(head_shape)
        raw_scores = jnp.einsum('slhe,smhe->shlm', queries, key_rows, precision=PRECISE)
        attention = jax.nn.softmax(low_back(raw_scores * score_scale), axis=-1)
        attended = jnp.einsum('shlm,smhe->slhe', low(attention), value_rows, precision=PRECISE)
        attended = rounded_both(attended.reshape(-1, D))
        branch_one = low_back(jnp.dot(attended, w_out[layer_at], precision=PRECISE) + b_out[layer_at])
        middle = residual + factors[:, 2] * branch_one
        normed_mid = low(layer_norm(middle) * (1.0 + factors[:, 4]) + factors[:, 3])
        up_proj = low_back(jnp.dot(normed_mid, w_up[layer_at], precision=PRECISE) + b_up[layer_at])
        activated = low(jax.nn.gelu(up_proj, approximate=True))
        branch_two = low_back(jnp.dot(activated, w_down[layer_at], precision=PRECISE) + b_down[layer_at])
        residual = middle + factors[:, 5] * branch_two
    return residual

def reference(latents, labels, step_ids, class_table, step_table, w_ada, b_ada, w_qkv, b_qkv, w_out, b_out, w_up, b_up, w_down, b_down, cotangent):

    def forward_all(rows_in, class_rows, step_rows, ada_weight, ada_bias, qkv_weight, qkv_bias, out_weight, out_bias, up_weight, up_bias, down_weight, down_bias):
        condition = class_rows[labels] + step_rows[step_ids]
        modulation = jnp.einsum('bd,ldjf->bljf', jax.nn.silu(condition), ada_weight, precision=PRECISE) + ada_bias[None]
        grouped = rows_in.reshape(N_DP, -1, D)
        group_mods = modulation.reshape(N_DP, -1, LAYERS, 6, D)

        def one_group(group_item):
            per_token = jnp.repeat(group_item[1], LENGTH, axis=0)
            return two_blocks(group_item[0], per_token, qkv_weight, qkv_bias, out_weight, out_bias, up_weight, up_bias, down_weight, down_bias)
        return lax.map(one_group, (grouped, group_mods)).reshape(-1, D)
    floats = [item.astype(jnp.float32) for item in (latents, class_table, step_table, w_ada, b_ada, w_qkv, b_qkv, w_out, b_out, w_up, b_up, w_down, b_down)]
    output, pullback = jax.vjp(forward_all, *floats)
    grads = pullback(cotangent.astype(jnp.float32))
    return (output.astype(jnp.bfloat16), grads[0].astype(jnp.bfloat16), grads[1], grads[2], grads[3], grads[4], grads[5], grads[6], grads[7], grads[8], grads[9], grads[10], grads[11], grads[12])
```

```python
import jax
import jax.numpy as jnp
from jax import lax
from jax.experimental import pallas as pl
from jax.experimental.pallas import tpu as pltpu
from jax.sharding import PartitionSpec as P

HEAD_DIM = 64
LENGTH = 256
PRECISE = lax.Precision.HIGHEST
NORM_EPSILON = 1e-06
F32 = jnp.float32
BF16 = jnp.bfloat16
ALL = ("dp", "row", "col")
GELU_A = 0.7978845608028654
GELU_B = 0.044715

COL_OF = (0, 3, 1, 2)
DP_OF = (0, 2, 3, 1)
ROUND_ONE = ((0, 2), (3, 1), (1, 3), (2, 0))
ROUND_TWO = (((0, 1), (2, 3)), ((3, 2), (1, 0)), ((1, 0), (3, 2)), ((2, 3), (0, 1)))


def dot(left, right):
    return lax.dot_general(left, right, (((1,), (0,)), ((), ())), preferred_element_type=F32)


def dot_t(left, right):
    return lax.dot_general(left, right, (((1,), (1,)), ((), ())), preferred_element_type=F32)


def t_dot(left, right):
    return lax.dot_general(left, right, (((0,), (0,)), ((), ())), preferred_element_type=F32)


def call(kernel, outs, *args, flops=0):
    total = sum(a.size * a.dtype.itemsize for a in args)
    total += sum(s[0][0] * 4 for s in outs)
    return pl.pallas_call(
        kernel,
        out_shape=[jax.ShapeDtypeStruct(shape, dtype) for shape, dtype in outs],
        compiler_params=pltpu.CompilerParams(vmem_limit_bytes=24 * 1024 * 1024),
        cost_estimate=pl.CostEstimate(flops=flops, bytes_accessed=total, transcendentals=0),
    )(*args)


def layer_norm(values):
    center = values - jnp.mean(values, axis=1, keepdims=True)
    inverse = lax.rsqrt(jnp.mean(center * center, axis=1, keepdims=True) + NORM_EPSILON)
    return center * inverse, inverse


def norm_back(grad, normed, inverse):
    return inverse * (
        grad
        - jnp.mean(grad, axis=1, keepdims=True)
        - normed * jnp.mean(grad * normed, axis=1, keepdims=True)
    )


def pick(index, values):
    chosen = jnp.int32(values[0])
    for at, value in enumerate(values[1:], 1):
        chosen = jnp.where(index == at, jnp.int32(value), chosen)
    return chosen


def after(value, *earlier):
    return lax.optimization_barrier((value,) + earlier)[0]


def column_sum(values):
    return jnp.sum(values, axis=0, keepdims=True)


def first_kernel(tokens_ref, mod_ref, out_ref):
    normed, _ = layer_norm(tokens_ref[0].astype(F32))
    out_ref[0] = (normed * (1.0 + mod_ref[1:2, :]) + mod_ref[0:1, :]).astype(BF16)
    out_ref[1] = (mod_ref[5:6, :] * tokens_ref[1].astype(F32)).astype(BF16)


def store_split(keep_ref, send_ref, which, first, second):
    rows, half = first.shape[0] // 2, first.shape[1]
    keep_ref[which, :, :half] = first[:rows]
    keep_ref[which, :, half:] = second[:rows]
    send_ref[which, :, :half] = first[rows:].astype(BF16)
    send_ref[which, :, half:] = second[rows:].astype(BF16)


def unfold(w):
    width = w.shape[1] // 3
    half, cut = 2 * width, 2 * width // 3
    top = jnp.concatenate([w[half : half + cut, :width], w[half : half + cut, width : 2 * width]], axis=1)
    low = w[half : half + cut, 2 * width :]
    low = jnp.concatenate([low[: cut // 2], low[cut // 2 :]], axis=1)
    return jnp.concatenate([top, low], axis=0)


def attention_kernel(a0, a1, b0, b1, wm, wo, hid_ref, dm_ref, oqkv_ref, p_ref, keep_ref, send_ref):
    width = wm.shape[1] // 3
    half = 2 * width
    cut = 2 * width // 3
    heads = width // HEAD_DIM
    bias = wm[half + cut : half + cut + 1, :].astype(F32)
    outm, outo = unfold(wm), unfold(wo)
    for which, (first, second) in enumerate(((a0, a1), (b0, b1))):
        rows = slice(which * LENGTH, (which + 1) * LENGTH)
        hidden = jnp.concatenate([first[0], second[0]], axis=0)
        hid_ref[rows, :] = hidden
        dm_ref[rows, :] = jnp.concatenate([first[1], second[1]], axis=0)
        qkv = (dot(hidden[:, :half], wm[:half, :]) + dot(hidden[:, half:], wo[:half, :]) + bias).astype(BF16)
        parts = []
        for head in range(heads):
            at = head * HEAD_DIM
            q = qkv[:, at : at + HEAD_DIM]
            k = qkv[:, width + at : width + at + HEAD_DIM]
            v = qkv[:, 2 * width + at : 2 * width + at + HEAD_DIM]
            scores = dot_t(q, k) * HEAD_DIM ** (-0.5)
            powers = jnp.exp(scores - jnp.max(scores, axis=1, keepdims=True))
            soft = powers * (1.0 / jnp.sum(powers, axis=1, keepdims=True))
            p_ref[which * heads + head] = soft
            parts.append(dot(soft.astype(BF16), v))
        attended = jnp.concatenate(parts, axis=1).astype(BF16)
        oqkv_ref[rows, :] = jnp.concatenate([attended, qkv], axis=1)
        store_split(keep_ref, send_ref, which, dot(attended, outm), dot(attended, outo))


def second_norm_kernel(keep, recv, recv_x, x_ref, mod_ref, a_ref, x1_ref, h_ref):
    branch = keep[0] + recv[0].astype(F32) + recv_x[...].astype(F32) + mod_ref[6:7, :]
    middle = x_ref[0].astype(F32) + mod_ref[2:3, :] * branch
    normed, _ = layer_norm(middle)
    a_ref[...] = branch
    x1_ref[...] = middle
    h_ref[...] = (normed * (1.0 + mod_ref[4:5, :]) + mod_ref[3:4, :]).astype(BF16)


def mlp_kernel(a0, a1, b0, b1, dm_ref, wm, wo, keep_ref, send_ref, mkeep, msend, gkeep, gsend):
    half = wm.shape[1]
    hid = 2 * half
    bias = jnp.concatenate([wm[2 * hid : 2 * hid + 1, :], wm[2 * hid + 1 : 2 * hid + 2, :]], axis=1)
    bias = bias.astype(F32)
    hiddens, acts, dups = [], [], []
    for which, (first, second) in enumerate(((a0, a1), (b0, b1))):
        rows = slice(which * LENGTH, (which + 1) * LENGTH)
        hidden = jnp.concatenate([first[...], second[...]], axis=0)
        up = [
            dot(hidden[:, :half], wm[s : s + half, :]) + dot(hidden[:, half:], wo[s : s + half, :])
            for s in (0, half)
        ]
        up = jnp.concatenate(up, axis=1) + bias
        square = up * up
        tanh = jnp.tanh(GELU_A * (up + GELU_B * up * square))
        act = (0.5 * up * (1.0 + tanh)).astype(BF16)
        slope = 0.5 * (1.0 + tanh) + 0.5 * up * (1.0 - tanh * tanh) * (
            GELU_A * (1.0 + 3.0 * GELU_B * square)
        )
        dm = dm_ref[rows, :]
        dg = dot_t(dm[:, :half], wm[hid : 2 * hid, :]) + dot_t(dm[:, half:], wo[hid : 2 * hid, :])
        du = (dg * slope).astype(BF16)
        back = [
            dot_t(du[:, :half], w[:half, :]) + dot_t(du[:, half:], w[half:hid, :])
            for w in (wm, wo)
        ]
        store_split(keep_ref, send_ref, which, back[0], back[1])
        store_split(mkeep, msend, which, dot(act, wm[hid : 2 * hid, :]), dot(act, wo[hid : 2 * hid, :]))
        hiddens.append(hidden)
        acts.append(act)
        dups.append(du)
    hidden, act, du = (jnp.concatenate(v, axis=0) for v in (hiddens, acts, dups))
    dm = dm_ref[...]
    for s in (0, half):
        gsend[s : s + half, :] = t_dot(hidden[:, half:], du[:, s : s + half]).astype(BF16)
        gkeep[s : s + half, :] = t_dot(hidden[:, :half], du[:, s : s + half])
    gsend[hid : 2 * hid, :] = t_dot(act, dm[:, half:]).astype(BF16)
    gkeep[hid : 2 * hid, :] = t_dot(act, dm[:, :half])
    bias = column_sum(du.astype(F32))
    bias = jnp.concatenate([bias[:, :half], bias[:, half:], jnp.zeros((14, half), F32)], axis=0)
    gkeep[2 * hid : 2 * hid + 16, :] = bias
    gsend[2 * hid : 2 * hid + 16, :] = bias.astype(BF16)


def second_back_kernel(keep, recv, recv_x, x1_ref, a_ref, ct_ref, dm_ref, mod_ref, da_ref, dx1_ref, sums_ref):
    dh = keep[0] + recv[0].astype(F32) + recv_x[...].astype(F32)
    normed, inverse = layer_norm(x1_ref[...])
    dx1 = ct_ref[1].astype(F32) + norm_back(dh * (1.0 + mod_ref[4:5, :]), normed, inverse)
    da = (mod_ref[2:3, :] * dx1).astype(BF16)
    dx1_ref[...] = dx1
    da_ref[...] = da
    sums_ref[0:1, :] = column_sum(dx1 * a_ref[...])
    sums_ref[1:2, :] = column_sum(dh)
    sums_ref[2:3, :] = column_sum(dh * normed)
    sums_ref[3:4, :] = column_sum(dm_ref[1].astype(F32))
    sums_ref[4:5, :] = column_sum(da.astype(F32))
    sums_ref[5:8, :] = jnp.zeros((3, sums_ref.shape[1]), F32)


def attention_back_kernel(
    hid_ref, da0, da1, db0, db1, oqkv_ref, p_ref, wm, wo, keep_ref, send_ref, gkeep, gsend
):
    width = wm.shape[1] // 3
    half = 2 * width
    cut = 2 * width // 3
    outm, outo = unfold(wm), unfold(wo)
    heads = width // HEAD_DIM
    scale = HEAD_DIM ** (-0.5)
    das, dqkvs = [], []
    for which, (first, second) in enumerate(((da0, da1), (db0, db1))):
        rows = slice(which * LENGTH, (which + 1) * LENGTH)
        da = jnp.concatenate([first[...], second[...]], axis=0)
        do = (dot_t(da[:, :half], outm) + dot_t(da[:, half:], outo)).astype(BF16)
        qkv = oqkv_ref[rows, width:]
        dqs, dks, dvs = [], [], []
        for head in range(heads):
            at = head * HEAD_DIM
            q = qkv[:, at : at + HEAD_DIM]
            k = qkv[:, width + at : width + at + HEAD_DIM]
            v = qkv[:, 2 * width + at : 2 * width + at + HEAD_DIM]
            do_head = do[:, at : at + HEAD_DIM]
            soft = p_ref[which * heads + head]
            dsoft = dot_t(do_head, v)
            ds = (soft * (dsoft - jnp.sum(soft * dsoft, axis=1, keepdims=True))).astype(BF16)
            dqs.append(dot(ds, k) * scale)
            dks.append(t_dot(ds, q) * scale)
            dvs.append(t_dot(soft.astype(BF16), do_head))
        dqkv = jnp.concatenate(dqs + dks + dvs, axis=1).astype(BF16)
        store_split(keep_ref, send_ref, which, dot_t(dqkv, wm[:half, :]), dot_t(dqkv, wo[:half, :]))
        das.append(da)
        dqkvs.append(dqkv)
    hidden = hid_ref[...]
    da = jnp.concatenate(das, axis=0)
    dqkv = jnp.concatenate(dqkvs, axis=0)
    o = oqkv_ref[:, :width]
    bias = jnp.pad(column_sum(dqkv.astype(F32)), ((0, 15), (0, 0)))
    for ref, side in ((gkeep, slice(0, half)), (gsend, slice(half, 2 * half))):
        ref[:half, :] = t_dot(hidden[:, side], dqkv).astype(ref.dtype)
        out = t_dot(o, da[:, side])
        low = jnp.concatenate([out[cut:, :width], out[cut:, width:]], axis=0)
        ref[half : half + cut, :] = jnp.concatenate(
            [out[:cut, :width], out[:cut, width:], low], axis=1
        ).astype(ref.dtype)
        ref[half + cut : half + cut + 16, :] = bias.astype(ref.dtype)


def last_kernel(
    keep, recv, recv_x, x_ref, dx1_ref, mod_ref, x1_ref, mkeep, mrecv, mrecv_x, two_ref, out_ref, sums_ref
):
    dh = keep[0] + recv[0].astype(F32) + recv_x[...].astype(F32)
    normed, inverse = layer_norm(x_ref[0].astype(F32))
    dx = dx1_ref[...] + norm_back(dh * (1.0 + mod_ref[1:2, :]), normed, inverse)
    branch = mkeep[0] + mrecv[0].astype(F32) + mrecv_x[...].astype(F32) + mod_ref[7:8, :]
    out_ref[0] = (x1_ref[...] + mod_ref[5:6, :] * branch).astype(BF16)
    out_ref[1] = dx.astype(BF16)
    sums_ref[0:1, :] = column_sum(dh)
    sums_ref[1:2, :] = column_sum(dh * normed)
    sums_ref[2:5, :] = two_ref[0:3, :]
    sums_ref[5:6, :] = column_sum(x_ref[1].astype(F32) * branch)
    sums_ref[6:8, :] = two_ref[3:5, :]


def make_body(n_dp, n_row, n_col):
    def flat(d, r, c):
        return (d * n_row + r) * n_col + c

    places = [(d, r, c) for d in range(n_dp) for r in range(n_row) for c in range(n_col)]

    def core_swap(v):
        return lax.ppermute(v, "dp", [(d, d ^ 1) for d in range(n_dp)])

    def chip_swap(v):
        return lax.ppermute(v, "dp", [(d, d ^ 2) for d in range(n_dp)])

    def row_swap(v):
        return lax.ppermute(v, "row", [(0, 1), (1, 0)])

    def shift(v, k):
        return lax.ppermute(v, "col", [(c, (c + k) % n_col) for c in range(n_col)])

    def col_swap(v, bit):
        return lax.ppermute(v, "col", [(c, c ^ bit) for c in range(n_col)])

    def spread(own):
        far = chip_swap(own)
        return (own, core_swap(own), far, core_swap(far))

    def gather_sum(keep, send):
        recv = core_swap(send)
        far = chip_swap((keep[1] + recv[1].astype(F32)).astype(BF16))
        return keep, recv, far

    def body(
        latents,
        labels,
        step_ids,
        class_table,
        step_table,
        w_ada,
        b_ada,
        w_qkv,
        b_qkv,
        w_out,
        b_out,
        w_up,
        b_up,
        w_down,
        b_down,
        cotangent,
    ):
        tokens, width_row = latents.shape
        per_block = tokens // LENGTH
        sequences = labels.shape[0]
        width = class_table.shape[1]
        half = width // 2
        cols = w_qkv.shape[3]
        hid = w_up.shape[2]
        cond_cols = w_ada.shape[1]
        quick = n_row == 2 and per_block == 1
        dp_at = lax.axis_index("dp")
        row_at = lax.axis_index("row")
        col_at = lax.axis_index("col")
        core_at = dp_at % 2
        owner = core_at == row_at % 2
        block = LENGTH // 2

        def gather_owner(own, other):
            across = lax.ppermute(
                own, ALL, [(flat(d, r, c), flat(d, 1 - r, c)) for d, r, c in places if d % 2 != r]
            )
            across_core = lax.ppermute(
                other, ALL, [(flat(d, r, c), flat(d ^ 1, 1 - r, c)) for d, r, c in places if d % 2 != r]
            )
            core = lax.ppermute(
                other, ALL, [(flat(d, r, c), flat(d ^ 1, r, c)) for d, r, c in places if d % 2 == r]
            )
            return jnp.concatenate(
                [jnp.where(owner, own, core), jnp.where(owner, across, across_core)], axis=-1
            )

        def tokens_in(v):
            if quick:
                own = lax.dynamic_slice_in_dim(v, core_at * block, block, 1)
                other = lax.dynamic_slice_in_dim(v, (1 - core_at) * block, block, 1)
                return gather_owner(own, other)
            full = lax.all_gather(v, "row", axis=2, tiled=True)
            full = jnp.where(owner, full, core_swap(full))
            return lax.dynamic_slice_in_dim(full, (row_at // 2) * LENGTH + core_at * block, block, 1)

        def tokens_out(v):
            if quick:
                mine, theirs = v[:, :, :half], v[:, :, half:]
                core = lax.ppermute(
                    mine, ALL, [(flat(d, r, c), flat(d ^ 1, r, c)) for d, r, c in places if d % 2 != r]
                )
                across = lax.ppermute(
                    theirs, ALL, [(flat(d, r, c), flat(d, 1 - r, c)) for d, r, c in places if d % 2 == r]
                )
                across_core = lax.ppermute(
                    theirs, ALL, [(flat(d, r, c), flat(d ^ 1, 1 - r, c)) for d, r, c in places if d % 2 != r]
                )
                first = jnp.where(owner, mine, across)
                second = jnp.where(owner, core, across_core)
                return jnp.where(
                    core_at == 0,
                    jnp.concatenate([first, second], axis=1),
                    jnp.concatenate([second, first], axis=1),
                )
            other = lax.ppermute(
                v, ALL, [(flat(d, r, c), flat(d ^ 1, r, c)) for d, r, c in places if d % 2 != r % 2]
            )
            full = jnp.where(
                core_at == 0, jnp.concatenate([v, other], axis=1), jnp.concatenate([other, v], axis=1)
            )
            rows = lax.all_gather(full, "row", axis=1)
            rows = rows.reshape(2, n_row // 2, 2, LENGTH, width)
            rows = lax.dynamic_index_in_dim(rows, core_at, 2, keepdims=False)
            rows = rows.reshape(2, tokens, width)
            return lax.dynamic_slice_in_dim(rows, row_at * width_row, width_row, 2)

        def first_round(v):
            return lax.ppermute(
                v,
                ALL,
                [
                    (flat(d, r, ROUND_ONE[d][0]), flat(d, r, ROUND_ONE[d][1]))
                    for d in range(n_dp)
                    for r in range(n_row)
                ],
            )

        def pack_attention(w, out):
            bias = jnp.concatenate([b_qkv[0, 0], jnp.zeros((cols,), BF16), b_qkv[0, 1]])
            cut = 2 * cols // 3
            folded = jnp.concatenate(
                [out[:cut, :cols], out[:cut, cols:], jnp.concatenate([out[cut:, :cols], out[cut:, cols:]], axis=0)],
                axis=1,
            )
            return jnp.concatenate([w, folded, jnp.pad(bias[None], ((0, 15), (0, 0)))], axis=0)

        source = pick(dp_at, COL_OF)
        relay = pick(dp_at, [pair[1] for pair in ROUND_ONE])
        at_source = col_at == source
        at_relay = col_at == relay

        def second_round(held):
            return lax.ppermute(
                held,
                ALL,
                [
                    (flat(d, r, a), flat(d, r, b))
                    for d in range(n_dp)
                    for r in range(n_row)
                    for a, b in ROUND_TWO[d]
                ],
            )

        def settle(held, second):
            return jnp.where(at_source | at_relay, held, second)

        if quick:
            own_att = pack_attention(w_qkv[0].reshape(width_row, 3 * cols), w_out[0])
            att_first = first_round(own_att)
            labels = after(labels, own_att)
        class_rows = class_table.shape[0]
        step_rows = step_table.shape[0]

        def hot(ids, rows):
            return ids[:, None] == (col_at * rows + jnp.arange(rows, dtype=jnp.int32))[None, :]

        partial_cond = dot(hot(labels, class_rows).astype(BF16), class_table) + dot(
            hot(step_ids, step_rows).astype(BF16), step_table
        )
        ada = w_ada[0].reshape(cond_cols, 6 * width_row).astype(F32)
        small_bias = jnp.concatenate([b_ada[0], b_out, b_down], axis=0).astype(F32)
        if quick:
            condition = (partial_cond + shift(partial_cond, 1)) + (
                shift(partial_cond, 2) + shift(partial_cond, 3)
            )
        else:
            condition = lax.psum(partial_cond, "col")
        cond_part = lax.dynamic_slice_in_dim(condition, col_at * cond_cols, cond_cols, 1)
        act_part = cond_part * jax.nn.sigmoid(cond_part)
        if quick:
            att_held = jnp.where(at_source, own_att, att_first)
            act_part = after(act_part, att_held)
            att_second = second_round(att_held)
        mod_part = jnp.dot(act_part, ada, precision=PRECISE)
        if quick:
            twice = jnp.concatenate([mod_part, mod_part], axis=0)
            turned = lax.dynamic_slice_in_dim(twice, col_at, n_col, 0)
            modulation = turned[0] + shift(turned[1], 1) + shift(turned[2], 2) + shift(turned[3], 3)
            modulation = modulation.reshape(6, width_row)
            mod_sum = modulation
            modulation = jnp.concatenate([modulation, jnp.zeros((2, width_row), F32)], axis=0)
            modulation = modulation + small_bias
            modulation = gather_owner(modulation, modulation)
        else:
            all_mod = lax.psum(mod_part, "col").reshape(sequences, 6, width_row)
            all_mod = jnp.concatenate([all_mod, jnp.zeros((sequences, 2, width_row), F32)], axis=1)
            all_mod = lax.all_gather(all_mod + small_bias[None], "row", axis=2, tiled=True)
            all_mod = jnp.where(owner, all_mod, core_swap(all_mod))
            modulation = lax.dynamic_index_in_dim(
                all_mod, col_at * per_block + row_at // 2, 0, keepdims=False
            )

        def pack_mlp(up, down):
            bias = jnp.pad(b_up.reshape(2, half), ((0, 14), (0, 0)))
            return jnp.concatenate([up[:, :half], up[:, half:], down, bias], axis=0)

        own_tokens = tokens_in(jnp.stack([latents, cotangent]))
        if quick:
            own_mlp = after(pack_mlp(w_up[0], w_down[0]), mod_sum)
            mlp_first = first_round(own_mlp)
            att_m = settle(att_held, att_second)
            modulation = after(modulation, att_m)
            att_o = row_swap(att_m)
        else:

            def fetch_whole(halves):
                taken = [
                    lax.dynamic_index_in_dim(lax.all_gather(v, "col"), source, 0, keepdims=False)
                    for v in halves
                ]
                return taken[0], taken[1]

            full_qkv = lax.all_gather(w_qkv[0].reshape(width_row, 3 * cols), "row", axis=0, tiled=True)
            full_out = lax.all_gather(w_out[0], "row", axis=1, tiled=True)
            full_up = lax.all_gather(w_up[0], "row", axis=0, tiled=True)
            full_down = lax.all_gather(w_down[0], "row", axis=1, tiled=True)
            att_m, att_o = fetch_whole(
                [pack_attention(full_qkv[:half], full_out[:, :half]), pack_attention(full_qkv[half:], full_out[:, half:])]
            )
            mlp_m, mlp_o = fetch_whole(
                [pack_mlp(full_up[:half], full_down[:, :half]), pack_mlp(full_up[half:], full_down[:, half:])]
            )

        heads = cols // HEAD_DIM
        shard = (block, width)
        pair = (2, block, width)
        both = 2 * LENGTH
        (first_own,) = call(first_kernel, [(pair, BF16)], own_tokens, modulation)
        first_all = spread(first_own)
        if quick:
            mlp_held = jnp.where(at_source, own_mlp, after(mlp_first, first_own))
            first_all = first_all[:3] + (after(first_all[3], mlp_held),)
            mlp_second = second_round(mlp_held)
        hidden_all, dm_all, oqkv, soft, keep, send = call(
            attention_kernel,
            [
                ((both, width), BF16),
                ((both, width), BF16),
                ((both, 4 * cols), BF16),
                ((2 * heads, LENGTH, LENGTH), F32),
                (pair, F32),
                (pair, BF16),
            ],
            *first_all,
            att_m,
            att_o,
            flops=2 * both * width * 4 * cols,
        )
        if quick:
            mlp_m = settle(mlp_held, after(mlp_second, first_all[3]))
            send = after(send, mlp_m)
            mlp_o = row_swap(mlp_m)
        branch_one, middle, hm_own = call(
            second_norm_kernel,
            [(shard, F32), (shard, F32), (shard, BF16)],
            *gather_sum(keep, send),
            own_tokens,
            modulation,
        )
        hm_all = spread(hm_own)

        def collect_one(keep, recv):
            total = keep + recv.astype(F32)
            return total, lax.ppermute(
                total.astype(BF16),
                ALL,
                [
                    (flat(d, r, b), flat(d, r, a))
                    for d in range(n_dp)
                    for r in range(n_row)
                    for a, b in ROUND_TWO[d]
                ],
            )

        def collect_two(total, recv):
            total = total + recv.astype(F32)
            return total, lax.ppermute(
                total.astype(BF16),
                ALL,
                [
                    (flat(d, r, ROUND_ONE[d][1]), flat(d, r, ROUND_ONE[d][0]))
                    for d in range(n_dp)
                    for r in range(n_row)
                ],
            )

        home = (pick(col_at, DP_OF) // 2) == (dp_at // 2)

        def collect_three(total, recv):
            total = (total + recv.astype(F32)).astype(BF16)
            return total, lax.ppermute(
                total,
                ALL,
                [
                    (flat(DP_OF[c], r, c), flat(DP_OF[c] ^ 2, r, c))
                    for r in range(n_row)
                    for c in range(n_col)
                ],
            )

        def collect_last(total, far):
            total = jnp.where(at_source, total, far)
            near = lax.ppermute(
                total,
                ALL,
                [
                    (flat(d, r, c), flat(d ^ 1, r, c))
                    for r in range(n_row)
                    for c in range(n_col)
                    for d in (DP_OF[c], DP_OF[c] ^ 2)
                ],
            )
            return jnp.where((dp_at % 2) == pick(col_at, DP_OF) % 2, total, near).astype(F32)

        n_mlp = 2 * hid + 16
        keep, send, mkeep, msend, mlp_keep, mlp_send = call(
            mlp_kernel,
            [
                (pair, F32),
                (pair, BF16),
                (pair, F32),
                (pair, BF16),
                ((n_mlp, half), F32),
                ((n_mlp, half), BF16),
            ],
            *hm_all,
            dm_all,
            mlp_m,
            mlp_o,
            flops=12 * both * width * hid,
        )
        hidden_sum = gather_sum(keep, send)
        da_own, dmiddle, sums_two = call(
            second_back_kernel,
            [(shard, BF16), (shard, F32), ((8, width), F32)],
            *hidden_sum,
            middle,
            branch_one,
            own_tokens,
            first_own,
            modulation,
        )
        da_all = spread(da_own)
        if quick:
            mlp_parts = collect_one(mlp_keep, after(row_swap(mlp_send), da_own))
            da_all = da_all[:3] + (after(da_all[3], mlp_parts[0]),)
        branch_sum = gather_sum(mkeep, after(msend, da_own))
        n_att = att_m.shape[0]
        keep, send, att_keep, att_send = call(
            attention_back_kernel,
            [(pair, F32), (pair, BF16), ((n_att, 3 * cols), F32), ((n_att, 3 * cols), BF16)],
            hidden_all,
            *da_all,
            oqkv,
            soft,
            att_m,
            att_o,
            flops=4 * both * width * 4 * cols,
        )
        input_sum = gather_sum(keep, send)
        if quick:
            mlp_parts = collect_two(mlp_parts[0], after(mlp_parts[1], send))
            input_sum = input_sum[:2] + (after(input_sum[2], mlp_parts[0]),)
            att_recv = row_swap(att_send)
        results, sums = call(
            last_kernel,
            [(pair, BF16), ((8, width), F32)],
            *input_sum,
            own_tokens,
            dmiddle,
            modulation,
            middle,
            *branch_sum,
            sums_two,
        )

        results = tokens_out(results)

        ids = jnp.stack([labels, step_ids], axis=1).astype(F32)
        if quick:
            small = jnp.concatenate([cond_part, ids], axis=1)
            near = core_swap(small)
            small = jnp.where(owner, jnp.stack([small, near]), jnp.stack([near, small]))
            small = jnp.stack([small, chip_swap(small)], axis=1).reshape(2, 2, 2, 2, cond_cols + 2)
            small = jnp.where(col_at % 2 == 1, small[:, :, :, ::-1], small)
            small = jnp.where(col_at >= 2, small[:, :, ::-1], small)
            small = small.transpose(2, 3, 0, 1, 4).reshape(n_dp * n_col, cond_cols + 2)
            all_cond = small[:, :cond_cols]
            all_ids = small[:, cond_cols:]
            sums = sums + core_swap(sums)
            far = chip_swap(sums)
            att_parts = collect_one(att_keep, after(att_recv, sums))
            far = after(far, att_parts[0])
            theirs = row_swap(jnp.concatenate([sums[:, half:], far[:, half:]], axis=0))
            mlp_parts = collect_three(mlp_parts[0], after(mlp_parts[1], far))
            theirs = after(theirs, mlp_parts[0])
            whole = jnp.concatenate([sums[:, :half], far[:, :half], theirs], axis=0)
            whole = jnp.concatenate([whole, col_swap(whole, 1)], axis=0)
            att_parts = collect_two(att_parts[0], after(att_parts[1], whole))
            whole = after(whole, att_parts[0])
            whole = [whole, col_swap(whole, 2)]
            dmod = jnp.concatenate(whole, axis=0).reshape(n_dp * n_col, 8, half)
        else:
            every = lax.all_gather(sums, ALL).reshape(2, 2, n_row // 2, 2, n_col, 8, width)
            every = jnp.sum(every, axis=1).transpose(0, 2, 3, 1, 4, 5)
            every = every.reshape(n_dp * sequences, 8, width)
            dmod = lax.dynamic_slice_in_dim(every, row_at * width_row, width_row, 2)
            all_cond = lax.all_gather(cond_part, "dp", axis=0, tiled=True)
            all_ids = lax.all_gather(ids, "dp", axis=0, tiled=True)

        gate = jax.nn.sigmoid(all_cond)
        all_act = all_cond * gate
        slope = gate * (1.0 + all_cond * (1.0 - gate))
        dmod_six = dmod[:, :6].reshape(-1, 6 * width_row)
        grad_ada = lax.dot_general(
            all_act, dmod_six, (((0,), (0,)), ((), ())), precision=PRECISE
        ).reshape(1, cond_cols, 6, width_row)
        totals = jnp.sum(dmod, axis=0)
        dact = lax.dot_general(dmod_six, ada, (((1,), (1,)), ((), ())), precision=PRECISE)
        if quick:
            flipped = row_swap(dact).reshape(n_col, 2, 2, cond_cols)[:, ::-1]
            att_parts = collect_three(att_parts[0], after(att_parts[1], dact))
            flipped = after(flipped, att_parts[0])
            dcond = slope * (dact + flipped.reshape(-1, cond_cols))
            dcond = dcond.reshape(n_col, n_dp, cond_cols)
            near = col_swap(dcond, 1)
            dcond = jnp.stack([dcond, near[jnp.array([1, 0, 3, 2])]])
            far = col_swap(dcond, 2)[:, jnp.array([2, 3, 0, 1])]
            around = jnp.stack([dcond, far])
            around = jnp.where(col_at % 2 == 1, around[:, ::-1], around)
            around = jnp.where(col_at >= 2, around[::-1], around)
            around = around.reshape(n_col, n_col, n_dp, cond_cols)
            dcond = around.transpose(1, 2, 0, 3).reshape(-1, width)
        else:
            dcond = slope * lax.psum(dact, "row")
            dcond = lax.all_gather(dcond, "col", axis=1, tiled=True)
        all_ids = all_ids.astype(jnp.int32)
        grad_class = lax.dot_general(
            hot(all_ids[:, 0], class_rows).astype(F32), dcond, (((0,), (0,)), ((), ())), precision=PRECISE
        )
        grad_step = lax.dot_general(
            hot(all_ids[:, 1], step_rows).astype(F32), dcond, (((0,), (0,)), ((), ())), precision=PRECISE
        )

        if quick:
            grad_mlp = collect_last(*mlp_parts)
            grad_att = collect_last(*att_parts)
        else:

            def collect_whole(keep, send):
                full = lax.psum(jnp.stack([keep, send.astype(F32)]), ("row", "col"))
                full = lax.all_gather(full, "dp")
                full = jnp.stack([full[d] for d in DP_OF])
                return lax.dynamic_index_in_dim(full, col_at, 0, keepdims=False)

            grad_mlp = collect_whole(mlp_keep, mlp_send)
            grad_att = collect_whole(att_keep, att_send)

        cut = 2 * cols // 3

        def take(v, dim):
            return lax.dynamic_slice_in_dim(v, row_at * width_row, width_row, dim)

        def split_attention(v):
            out = jnp.concatenate([v[half : half + cut, :cols], v[half : half + cut, cols : 2 * cols]], axis=1)
            low = v[half : half + cut, 2 * cols :]
            low = jnp.concatenate([low[: cut // 2], low[cut // 2 :]], axis=1)
            return v[:half], jnp.concatenate([out, low], axis=0)

        def split_mlp(v):
            return jnp.concatenate([v[:half], v[half:hid]], axis=1), v[hid : 2 * hid]

        if quick:
            grad_qkv, grad_out = split_attention(grad_att)
            grad_up, grad_down = split_mlp(grad_mlp)
            bias_att, bias_mlp = grad_att[half + cut], grad_mlp[2 * hid : 2 * hid + 2]
        else:
            first, second = split_attention(grad_att[0]), split_attention(grad_att[1])
            grad_qkv = take(jnp.concatenate([first[0], second[0]], axis=0), 0)
            grad_out = take(jnp.concatenate([first[1], second[1]], axis=1), 1)
            first, second = split_mlp(grad_mlp[0]), split_mlp(grad_mlp[1])
            grad_up = take(jnp.concatenate([first[0], second[0]], axis=0), 0)
            grad_down = take(jnp.concatenate([first[1], second[1]], axis=1), 1)
            bias_att, bias_mlp = grad_att[0, half + cut], grad_mlp[0, 2 * hid : 2 * hid + 2]
        grad_bias_qkv = jnp.stack([bias_att[:cols], bias_att[2 * cols :]])

        return (
            results[0],
            results[1],
            grad_class,
            grad_step,
            grad_ada,
            totals[None, :6],
            grad_qkv.reshape(1, width_row, 3, cols),
            grad_bias_qkv[None],
            grad_out[None],
            totals[None, 7],
            grad_up[None],
            bias_mlp.reshape(1, hid),
            grad_down[None],
            totals[None, 6],
        )

    return body


def solution(mesh):
    return jax.shard_map(
        make_body(mesh.shape["dp"], mesh.shape["row"], mesh.shape["col"]),
        mesh=mesh,
        in_specs=(
            P(("dp", "col"), "row"),
            P("dp"),
            P("dp"),
            P("col", None),
            P("col", None),
            P(None, "col", None, "row"),
            P(None, None, "row"),
            P(None, "row", None, "col"),
            P(None, None, "col"),
            P(None, "col", "row"),
            P(None, "row"),
            P(None, "row", "col"),
            P(None, "col"),
            P(None, "col", "row"),
            P(None, "row"),
            P(("dp", "col"), "row"),
        ),
        out_specs=(
            P(("dp", "col"), "row"),
            P(("dp", "col"), "row"),
            P("col", None),
            P("col", None),
            P(None, "col", None, "row"),
            P(None, None, "row"),
            P(None, "row", None, "col"),
            P(None, None, "col"),
            P(None, "col", "row"),
            P(None, "row"),
            P(None, "row", "col"),
            P(None, "col"),
            P(None, "col", "row"),
            P(None, "row"),
        ),
        check_vma=False,
    )
```

```python
import jax
import jax.numpy as jnp
from jax import lax
from jax.experimental import pallas as pl
from jax.experimental.pallas import tpu as pltpu
from jax.sharding import PartitionSpec as P

HEAD_DIM = 64
LENGTH = 256
PRECISE = lax.Precision.HIGHEST
NORM_EPSILON = 1e-06
F32 = jnp.float32
BF16 = jnp.bfloat16
ALL = ("dp", "row", "col")
GELU_A = 0.7978845608028654
GELU_B = 0.044715


def dot(left, right):
    return lax.dot_general(left, right, (((1,), (0,)), ((), ())), preferred_element_type=F32)


def dot_t(left, right):
    return lax.dot_general(left, right, (((1,), (1,)), ((), ())), preferred_element_type=F32)


def t_dot(left, right):
    return lax.dot_general(left, right, (((0,), (0,)), ((), ())), preferred_element_type=F32)


def call(kernel, outs, *args, scalar=None, flops=0, limit=28):
    total = sum(a.size * a.dtype.itemsize for a in args)
    total += sum(s[0][-1] * s[0][-2] * 4 for s in outs)
    specs = [pl.BlockSpec(memory_space=pltpu.VMEM)] * len(args)
    if scalar is not None:
        specs = [pl.BlockSpec(memory_space=pltpu.SMEM)] + specs
        args = (scalar,) + args
    return pl.pallas_call(
        kernel,
        in_specs=specs,
        out_specs=[pl.BlockSpec(memory_space=pltpu.VMEM)] * len(outs),
        out_shape=[jax.ShapeDtypeStruct(shape, dtype) for shape, dtype in outs],
        compiler_params=pltpu.CompilerParams(vmem_limit_bytes=limit * 1024 * 1024),
        cost_estimate=pl.CostEstimate(flops=flops, bytes_accessed=total, transcendentals=0),
    )(*args)


def layer_norm(values):
    center = values - jnp.mean(values, axis=1, keepdims=True)
    inverse = lax.rsqrt(jnp.mean(center * center, axis=1, keepdims=True) + NORM_EPSILON)
    return center * inverse, inverse


def norm_back(grad, normed, inverse):
    return inverse * (
        grad
        - jnp.mean(grad, axis=1, keepdims=True)
        - normed * jnp.mean(grad * normed, axis=1, keepdims=True)
    )


def pick(index, values):
    chosen = jnp.int32(values[0])
    for at, value in enumerate(values[1:], 1):
        chosen = jnp.where(index == at, jnp.int32(value), chosen)
    return chosen


def after(value, *earlier):
    return lax.optimization_barrier((value,) + earlier)[0]


def pieces_of(values):
    high = lax.reduce_precision(values, 8, 7)
    rest = values - high
    middle = lax.reduce_precision(rest, 8, 7)
    return jnp.stack([high, middle, rest - middle]).astype(BF16)


def column_sum(values):
    return jnp.sum(values, axis=0, keepdims=True)


def unfold(folded):
    rows = folded.shape[0] // 2
    return jnp.concatenate([folded[:rows], folded[rows:]], axis=1)


def fold(values):
    lanes = values.shape[1] // 2
    return jnp.concatenate([values[:, :lanes], values[:, lanes:]], axis=0)


def by_core(core_ref, body, mine, theirs):
    @pl.when(core_ref[0] == 0)
    def _():
        body(0, mine, theirs)

    @pl.when(core_ref[0] == 1)
    def _():
        body(1, theirs, mine)


def attention_kernel(
    core_ref, tok_ref, mod_ref, a0, a1, a2, a3, b_ref,
    hid_ref, oqkv_ref, p_ref, keep_ref, send_ref,
):
    half = a0.shape[1]
    width = half // 2
    heads = width // HEAD_DIM
    normed, _ = layer_norm(jnp.concatenate([tok_ref[0], tok_ref[2]], axis=0).astype(F32))
    hidden = (normed * (1.0 + mod_ref[1:2, :]) + mod_ref[0:1, :]).astype(BF16)
    hid_ref[...] = hidden

    def body(_, first, second):
        total_m = total_o = None
        blocks = (
            (first[0], second[0], first[2], second[2]),
            (first[1], second[1], first[3], second[3]),
        )
        for which, (qk_m, vo_m, qk_o, vo_o) in enumerate(blocks):
            left, right = hidden[:, :half], hidden[:, half:]
            qk = dot(left, qk_m[:half, :]) + dot(right, qk_o[:half, :])
            qk = (qk + qk_m[half : half + 1, :].astype(F32)).astype(BF16)
            v = dot(left, vo_m[:half, :width]) + dot(right, vo_o[:half, :width])
            v = (v + vo_m[half : half + 1, :width].astype(F32)).astype(BF16)
            parts = []
            for head in range(heads):
                at = head * HEAD_DIM
                scores = dot_t(qk[:, at : at + HEAD_DIM], qk[:, width + at : width + at + HEAD_DIM])
                scores = scores * HEAD_DIM ** (-0.5)
                powers = jnp.exp(scores - jnp.max(scores, axis=1, keepdims=True))
                soft = powers * (1.0 / jnp.sum(powers, axis=1, keepdims=True))
                p_ref[which * heads + head] = soft
                parts.append(dot(soft.astype(BF16), v[:, at : at + HEAD_DIM]))
            attended = jnp.concatenate(parts, axis=1).astype(BF16)
            oqkv_ref[:, which * 2 * half : (which + 1) * 2 * half] = jnp.concatenate([attended, qk, v], axis=1)
            part_m = dot(attended, unfold(vo_m[:half, width:]))
            part_o = dot(attended, unfold(vo_o[:half, width:]))
            total_m = part_m if total_m is None else total_m + part_m
            total_o = part_o if total_o is None else total_o + part_o
        split(keep_ref, send_ref, total_m, total_o)

    by_core(core_ref, body, (a0, a1, a2, a3), [b_ref.at[at] for at in range(4)])


def split(keep_ref, send_ref, first, second):
    rows, half = first.shape[0] // 2, first.shape[1]
    keep_ref[:, :half] = first[:rows]
    keep_ref[:, half:] = second[:rows]
    send_ref[:, :half] = first[rows:].astype(BF16)
    send_ref[:, half:] = second[rows:].astype(BF16)


def second_norm_kernel(keep, recv, x_ref, mod_ref, a_ref, x1_ref, h_ref):
    branch = keep[...] + recv[...].astype(F32) + mod_ref[6:7, :]
    middle = x_ref[0].astype(F32) + mod_ref[2:3, :] * branch
    normed, _ = layer_norm(middle)
    a_ref[...] = branch
    x1_ref[...] = middle
    h_ref[...] = (normed * (1.0 + mod_ref[4:5, :]) + mod_ref[3:4, :]).astype(BF16)


def mlp_kernel(
    h0, h1, tok_ref, mod_ref, a0, a1, a2, a3, b_ref, b3,
    keep_ref, send_ref, mkeep, msend, gkeep, gsend,
):
    half = a0.shape[1]
    hidden = jnp.concatenate([h0[...], h1[...]], axis=0)
    dm = jnp.concatenate([tok_ref[1], tok_ref[3]], axis=0).astype(F32) * mod_ref[5:6, :]
    dm = dm.astype(BF16)
    left, right = hidden[:, :half], hidden[:, half:]
    dleft, dright = dm[:, :half], dm[:, half:]
    sums = None
    for own, oth, grads, which in (
        (a0, a2, gkeep, 0),
        (a1, a3, gkeep, 1),
        (b_ref.at[0], b_ref.at[1], gsend, 0),
        (b_ref.at[2], b3, gsend, 1),
    ):
        up = dot(left, own[:half, :]) + dot(right, oth[:half, :])
        up = up + own[2 * half : 2 * half + 1, :].astype(F32)
        square = up * up
        tanh = jnp.tanh(GELU_A * (up + GELU_B * up * square))
        act = (0.5 * up * (1.0 + tanh)).astype(BF16)
        slope = 0.5 * (1.0 + tanh) + 0.5 * up * (1.0 - tanh * tanh) * (
            GELU_A * (1.0 + 3.0 * GELU_B * square)
        )
        dg = dot_t(dleft, own[half : 2 * half, :]) + dot_t(dright, oth[half : 2 * half, :])
        du = (dg * slope).astype(BF16)
        parts = (
            dot_t(du, own[:half, :]),
            dot_t(du, oth[:half, :]),
            dot(act, own[half : 2 * half, :]),
            dot(act, oth[half : 2 * half, :]),
        )
        sums = parts if sums is None else tuple(a + b for a, b in zip(sums, parts))
        bias = jnp.pad(column_sum(du.astype(F32)), ((0, 15), (0, 0))).astype(BF16)
        for side, (tokens, dtokens) in enumerate(((left, dleft), (right, dright))):
            grads[which, side, :half, :] = t_dot(tokens, du).astype(BF16)
            grads[which, side, half : 2 * half, :] = t_dot(act, dtokens).astype(BF16)
            grads[which, side, 2 * half : 2 * half + 16, :] = bias
    split(keep_ref, send_ref, sums[0], sums[1])
    split(mkeep, msend, sums[2], sums[3])


def second_back_kernel(keep, recv, x1_ref, a_ref, tok_ref, mod_ref, da_ref, dx1_ref, sums_ref):
    dh = keep[...] + recv[...].astype(F32)
    normed, inverse = layer_norm(x1_ref[...])
    dy = tok_ref[1].astype(F32)
    dx1 = dy + norm_back(dh * (1.0 + mod_ref[4:5, :]), normed, inverse)
    da = (mod_ref[2:3, :] * dx1).astype(BF16)
    dx1_ref[...] = dx1
    da_ref[...] = da
    sums_ref[0:1, :] = column_sum(dx1 * a_ref[...])
    sums_ref[1:2, :] = column_sum(dh)
    sums_ref[2:3, :] = column_sum(dh * normed)
    sums_ref[3:4, :] = column_sum((mod_ref[5:6, :] * dy).astype(BF16).astype(F32))
    sums_ref[4:5, :] = column_sum(da.astype(F32))
    sums_ref[5:8, :] = jnp.zeros((3, sums_ref.shape[1]), F32)


def attention_back_kernel(
    core_ref, hid_ref, da0, da1, oqkv_ref, p_ref, a0, a1, a2, a3, b_ref,
    keep_ref, send_ref, gkeep, gsend,
):
    half = a0.shape[1]
    width = half // 2
    heads = width // HEAD_DIM
    scale = HEAD_DIM ** (-0.5)
    hidden = hid_ref[...]
    da = jnp.concatenate([da0[...], da1[...]], axis=0)
    da_sides = (da[:, :half], da[:, half:])
    h_sides = (hidden[:, :half], hidden[:, half:])

    def body(core, first, second):
        pieces = (gkeep, gsend) if core == 0 else (gsend, gkeep)
        total_m = total_o = None
        blocks = (
            (first[0], second[0], first[2], second[2]),
            (first[1], second[1], first[3], second[3]),
        )
        for which, (qk_m, vo_m, qk_o, vo_o) in enumerate(blocks):
            base = which * 2 * half
            attended = oqkv_ref[:, base : base + width]
            qk = oqkv_ref[:, base + width : base + 3 * width]
            values = oqkv_ref[:, base + 3 * width : base + 4 * width]
            do = dot_t(da_sides[0], unfold(vo_m[:half, width:]))
            do = (do + dot_t(da_sides[1], unfold(vo_o[:half, width:]))).astype(BF16)
            dqs, dks, dvs = [], [], []
            for head in range(heads):
                at = head * HEAD_DIM
                q = qk[:, at : at + HEAD_DIM]
                k = qk[:, width + at : width + at + HEAD_DIM]
                do_head = do[:, at : at + HEAD_DIM]
                soft = p_ref[which * heads + head]
                dsoft = dot_t(do_head, values[:, at : at + HEAD_DIM])
                ds = (soft * (dsoft - jnp.sum(soft * dsoft, axis=1, keepdims=True))).astype(BF16)
                dqs.append(dot(ds, k) * scale)
                dks.append(t_dot(ds, q) * scale)
                dvs.append(t_dot(soft.astype(BF16), do_head))
            dqk = jnp.concatenate(dqs + dks, axis=1).astype(BF16)
            dv = jnp.concatenate(dvs, axis=1).astype(BF16)
            part_m = dot_t(dqk, qk_m[:half, :]) + dot_t(dv, vo_m[:half, :width])
            part_o = dot_t(dqk, qk_o[:half, :]) + dot_t(dv, vo_o[:half, :width])
            total_m = part_m if total_m is None else total_m + part_m
            total_o = part_o if total_o is None else total_o + part_o
            bias_qk = jnp.pad(column_sum(dqk.astype(F32)), ((0, 15), (0, 0))).astype(BF16)
            bias_v = jnp.pad(column_sum(dv.astype(F32)), ((0, 15), (0, width))).astype(BF16)
            for side in (0, 1):
                pieces[0][which, side, :half, :] = t_dot(h_sides[side], dqk).astype(BF16)
                pieces[0][which, side, half : half + 16, :] = bias_qk
                grad_v = t_dot(h_sides[side], dv)
                grad_o = fold(t_dot(attended, da_sides[side]))
                pieces[1][which, side, :half, :] = jnp.concatenate([grad_v, grad_o], axis=1).astype(BF16)
                pieces[1][which, side, half : half + 16, :] = bias_v
        split(keep_ref, send_ref, total_m, total_o)

    by_core(core_ref, body, (a0, a1, a2, a3), [b_ref.at[at] for at in range(4)])


def last_kernel(
    keep, recv, tok_ref, dx1_ref, mod_ref, x1_ref, mkeep, mrecv, two_ref, out_ref, sums_ref
):
    dh = keep[...] + recv[...].astype(F32)
    normed, inverse = layer_norm(tok_ref[0].astype(F32))
    dx = dx1_ref[...] + norm_back(dh * (1.0 + mod_ref[1:2, :]), normed, inverse)
    branch = mkeep[...] + mrecv[...].astype(F32) + mod_ref[7:8, :]
    out_ref[0] = (x1_ref[...] + mod_ref[5:6, :] * branch).astype(BF16)
    out_ref[1] = dx.astype(BF16)
    sums_ref[0:1, :] = column_sum(dh)
    sums_ref[1:2, :] = column_sum(dh * normed)
    sums_ref[2:5, :] = two_ref[0:3, :]
    sums_ref[5:6, :] = column_sum(tok_ref[1].astype(F32) * branch)
    sums_ref[6:8, :] = two_ref[3:5, :]


def make_body(n_dp, n_row, n_col):
    def flat(d, r, c):
        return (d * n_row + r) * n_col + c

    places = [(d, r, c) for d in range(n_dp) for r in range(n_row) for c in range(n_col)]

    def core_swap(v):
        return lax.ppermute(v, "dp", [(d, d ^ 1) for d in range(n_dp)])

    def chip_swap(v):
        return lax.ppermute(v, "dp", [(d, d ^ 2) for d in range(n_dp)])

    def row_swap(v):
        return lax.ppermute(v, "row", [(0, 1), (1, 0)])

    def col_swap(v, bits):
        return lax.ppermute(v, "col", [(c, c ^ bits) for c in range(n_col)])

    def total(*parts):
        out = parts[0].astype(F32)
        for part in parts[1:]:
            out = out + part.astype(F32)
        return out.astype(BF16)

    def body(
        latents,
        labels,
        step_ids,
        class_table,
        step_table,
        w_ada,
        b_ada,
        w_qkv,
        b_qkv,
        w_out,
        b_out,
        w_up,
        b_up,
        w_down,
        b_down,
        cotangent,
    ):
        tokens, width_row = latents.shape
        per_block = tokens // LENGTH
        sequences = labels.shape[0]
        width = class_table.shape[1]
        half = width // 2
        cols = w_qkv.shape[3]
        hid = w_up.shape[2]
        cond_cols = w_ada.shape[1]
        quick = n_row == 2 and per_block == 1
        dp_at = lax.axis_index("dp")
        row_at = lax.axis_index("row")
        col_at = lax.axis_index("col")
        core_at = dp_at % 2
        near_at = dp_at // 2
        block = LENGTH // 2
        core_arg = core_at.astype(jnp.int32).reshape(1)

        owner = near_at == row_at % 2

        def at_odd(condition, v, axis):
            return jnp.where(condition, jnp.flip(v, axis), v)

        def gather_owner(own, other, *earlier):
            across = lax.ppermute(
                own, ALL, [(flat(d, r, c), flat(d, 1 - r, c)) for d, r, c in places if d // 2 != r]
            )
            across_near = lax.ppermute(
                other, ALL, [(flat(d, r, c), flat(d ^ 2, 1 - r, c)) for d, r, c in places if d // 2 != r]
            )
            near = lax.ppermute(
                other, ALL, [(flat(d, r, c), flat(d ^ 2, r, c)) for d, r, c in places if d // 2 == r]
            )
            across = after(across, *earlier)
            return jnp.concatenate(
                [jnp.where(owner, own, near), jnp.where(owner, across, across_near)], axis=-1
            )

        def tokens_in(v):
            if quick:
                own = lax.dynamic_slice_in_dim(v, near_at * block, block, 1)
                other = lax.dynamic_slice_in_dim(v, (1 - near_at) * block, block, 1)
                return gather_owner(
                    jnp.concatenate([own, other], axis=0), jnp.concatenate([other, own], axis=0)
                )
            full = lax.all_gather(v, "row", axis=2, tiled=True)
            full = jnp.where(owner, full, chip_swap(full))
            start = (row_at // 2) * LENGTH
            own = lax.dynamic_slice_in_dim(full, start + near_at * block, block, 1)
            other = lax.dynamic_slice_in_dim(full, start + (1 - near_at) * block, block, 1)
            return jnp.concatenate([own, other], axis=0)

        def tokens_out(v):
            if quick:
                mine, theirs = v[:, :, :half], v[:, :, half:]
                near = lax.ppermute(
                    mine, ALL, [(flat(d, r, c), flat(d ^ 2, r, c)) for d, r, c in places if d // 2 != r]
                )
                across = lax.ppermute(
                    theirs, ALL, [(flat(d, r, c), flat(d, 1 - r, c)) for d, r, c in places if d // 2 == r]
                )
                across_near = lax.ppermute(
                    theirs, ALL, [(flat(d, r, c), flat(d ^ 2, 1 - r, c)) for d, r, c in places if d // 2 != r]
                )
                first = jnp.where(owner, mine, across)
                second = jnp.where(owner, near, across_near)
                return jnp.where(
                    near_at == 0,
                    jnp.concatenate([first, second], axis=1),
                    jnp.concatenate([second, first], axis=1),
                )
            other = chip_swap(v)
            full = jnp.where(
                near_at == 0, jnp.concatenate([v, other], axis=1), jnp.concatenate([other, v], axis=1)
            )
            rows = lax.all_gather(full, "row", axis=1)
            rows = rows.reshape(2, n_row // 2, 2, LENGTH, width)
            rows = lax.dynamic_index_in_dim(rows, near_at, 2, keepdims=False)
            rows = rows.reshape(2, tokens, width)
            return lax.dynamic_slice_in_dim(rows, row_at * width_row, width_row, 2)

        first_hop = [
            (flat(d, r, a), flat(d, r, b))
            for d in range(n_dp)
            for r in range(n_row)
            for a, b in (((0, 2), (3, 1)) if d // 2 == 0 else ((1, 3), (2, 0)))
        ]
        last_hop = [(b, a) for a, b in first_hop]
        held_at = jnp.where(near_at == 0, pick(col_at, (0, 3, 0, 3)), pick(col_at, (2, 1, 2, 1)))
        beside_at = jnp.where(near_at == 0, pick(col_at, (3, 0, 3, 0)), pick(col_at, (1, 2, 1, 2)))
        at_source = held_at == col_at

        def pack_attention(w, out):
            bias = jnp.concatenate(
                [b_qkv[0, 0], jnp.zeros((cols,), BF16), b_qkv[0, 1], jnp.zeros((cols,), BF16)]
            ).reshape(2, 1, 2 * cols)
            bias = jnp.pad(bias, ((0, 0), (0, 15), (0, 0)))
            second = jnp.concatenate([w[:, 2 * cols :], fold(out)], axis=1)
            return jnp.concatenate([jnp.stack([w[:, : 2 * cols], second]), bias], axis=1)

        def pack_mlp(up, down):
            bias = jnp.pad(b_up.reshape(2, 1, half), ((0, 0), (0, 15), (0, 0)))
            return jnp.concatenate(
                [jnp.stack([up[:, :half], up[:, half:]]), down.reshape(2, half, half), bias], axis=1
            )

        def by_piece(v):
            return jnp.where(core_at == 0, v[0], v[1]), jnp.where(core_at == 0, v[1], v[0])

        if quick:
            own_att = pack_attention(w_qkv[0].reshape(width_row, 3 * cols), w_out[0])
            piece = by_piece(own_att)[0]
            own_ids = jnp.stack([labels, step_ids], axis=1)
            other = chip_swap(own_ids)
            chips = jnp.where(near_at == 0, jnp.stack([own_ids, other]), jnp.stack([other, own_ids]))
            labels, step_ids = chips[:, :, 0].reshape(-1), chips[:, :, 1].reshape(-1)
            mlp_piece = by_piece(after(pack_mlp(w_up[0], w_down[0]), piece))[0]

        def to_chip(v):
            return lax.ppermute(
                v,
                ALL,
                [(flat(d, r, c), flat(d ^ 2, r, c)) for d, r, c in places if (d // 2 == 0) == (c in (0, 3))],
            )

        class_rows = class_table.shape[0]
        step_rows = step_table.shape[0]

        def hot(ids, rows):
            return ids[:, None] == (col_at * rows + jnp.arange(rows, dtype=jnp.int32))[None, :]

        partial_cond = dot(hot(labels, class_rows).astype(BF16), class_table) + dot(
            hot(step_ids, step_rows).astype(BF16), step_table
        )
        ada = w_ada[0]
        small_bias = jnp.concatenate([b_ada[0], b_out, b_down], axis=0).astype(F32)
        if quick:
            near = col_swap(partial_cond, 1)
            condition = (partial_cond + near) + (
                col_swap(partial_cond, 2) + col_swap(partial_cond, 3)
            )
        else:
            condition = lax.psum(partial_cond, "col")
        cond_part = lax.dynamic_slice_in_dim(condition, col_at * cond_cols, cond_cols, 1)
        act_part = cond_part * jax.nn.sigmoid(cond_part)
        if quick:
            own_tokens = tokens_in(after(jnp.stack([latents, cotangent]), condition))
            att_first = lax.ppermute(after(piece, condition), ALL, first_hop)
            held = jnp.where(at_source, piece, att_first)
            beside = col_swap(held, 1)
        mod_part = jnp.sum(
            jnp.einsum("pbd,djf->pbjf", pieces_of(act_part), ada, preferred_element_type=F32), axis=0
        ).reshape(act_part.shape[0], -1)
        if quick:
            turned = at_odd(col_at % 2 == 1, mod_part.reshape(2, 2, 2, -1), 2)
            turned = at_odd(col_at >= 2, turned, 1).reshape(2, n_col, -1)
            mod_sum = (turned[:, 0] + col_swap(turned[:, 1], 1)) + (
                col_swap(turned[:, 2], 2) + col_swap(turned[:, 3], 3)
            )
            mod_sum = after(mod_sum, held, own_tokens)
            both = jnp.concatenate([mod_sum.reshape(2, 6, width_row), jnp.zeros((2, 2, width_row), F32)], axis=1)
            both = both + small_bias[None]
            both = at_odd(row_at == 1, both, 0)
            other = row_swap(both[1])
            held_row = row_swap(after(held, other))
            beside_row = row_swap(after(beside, other))
            modulation = jnp.concatenate([both[0], other], axis=1)
        else:
            all_mod = lax.psum(mod_part, "col").reshape(sequences, 6, width_row)
            all_mod = jnp.concatenate([all_mod, jnp.zeros((sequences, 2, width_row), F32)], axis=1)
            all_mod = lax.all_gather(all_mod + small_bias[None], "row", axis=2, tiled=True)
            all_mod = jnp.where(owner, all_mod, chip_swap(all_mod))
            modulation = lax.dynamic_index_in_dim(
                all_mod, col_at * per_block + row_at // 2, 0, keepdims=False
            )

        def from_partner(mine):
            return core_swap(jnp.stack(mine))

        if quick:
            att_mine = (held, beside, held_row, beside_row)
            mlp_first = lax.ppermute(after(mlp_piece, beside), ALL, first_hop)
            held = jnp.where(at_source, mlp_piece, mlp_first)
            att_theirs = from_partner(att_mine[:3] + (after(att_mine[3], held),))
            beside = col_swap(held, 1)
            held_row = row_swap(held)
            own_tokens = after(own_tokens, beside, held_row)
            beside_row = row_swap(beside)
        else:
            own_tokens = tokens_in(jnp.stack([latents, cotangent]))
            full_qkv = lax.all_gather(w_qkv[0].reshape(width_row, 3 * cols), "row", axis=0, tiled=True)
            full_out = lax.all_gather(w_out[0], "row", axis=1, tiled=True)
            full_up = lax.all_gather(w_up[0], "row", axis=0, tiled=True)
            full_down = lax.all_gather(w_down[0], "row", axis=1, tiled=True)

            def fetch(first, second):
                every = lax.all_gather(jnp.stack([first, second]), "col")
                parts = [
                    by_piece(lax.dynamic_index_in_dim(every, at, 0, keepdims=False)[side])
                    for side in (0, 1)
                    for at in (held_at, beside_at)
                ]
                return tuple(v[0] for v in parts), jnp.stack([v[1] for v in parts])

            att_mine, att_theirs = fetch(
                pack_attention(full_qkv[:half], full_out[:, :half]),
                pack_attention(full_qkv[half:], full_out[:, half:]),
            )
            mlp_mine, mlp_theirs = fetch(
                pack_mlp(full_up[:half], full_down[:, :half]), pack_mlp(full_up[half:], full_down[:, half:])
            )
            mlp_theirs = mlp_theirs[jnp.array([0, 2, 1])], mlp_theirs[3]
        att_weights = att_mine + (att_theirs,)

        heads = 2 * cols // HEAD_DIM
        shard = (block, width)
        hidden_all, oqkv, soft, keep, send = call(
            attention_kernel,
            [
                ((LENGTH, width), BF16),
                ((LENGTH, 8 * cols), BF16),
                ((heads, LENGTH, LENGTH), F32),
                (shard, F32),
                (shard, BF16),
            ],
            own_tokens,
            modulation,
            *att_weights,
            scalar=core_arg,
            flops=2 * LENGTH * width * 8 * cols,
        )
        recv = chip_swap(send)
        branch_one, middle, hm_own = call(
            second_norm_kernel,
            [(shard, F32), (shard, F32), (shard, BF16)],
            keep,
            recv,
            own_tokens,
            modulation,
        )

        hm_far = chip_swap(hm_own)
        if quick:
            beside_row = after(beside_row, hm_far)
            mlp_mine = (held, beside, held_row, beside_row)
            mlp_theirs = from_partner((held, held_row, beside)), core_swap(beside_row)

        n_mlp = 2 * half + 16
        grads = ((2, 2, n_mlp, half), BF16)
        keep, send, mkeep, msend, mlp_keep, mlp_send = call(
            mlp_kernel,
            [(shard, F32), (shard, BF16), (shard, F32), (shard, BF16), grads, grads],
            hm_own,
            hm_far,
            own_tokens,
            modulation,
            *mlp_mine,
            *mlp_theirs,
            flops=24 * LENGTH * width * hid,
        )
        recv = chip_swap(send)
        if quick:
            mlp_sum = total(mlp_keep, after(core_swap(mlp_send), recv))
            recv = after(recv, mlp_sum)
            mlp_rows = row_swap(mlp_sum[:, 1])
        da_own, dmiddle, sums_two = call(
            second_back_kernel,
            [(shard, BF16), (shard, F32), ((8, width), F32)],
            keep,
            recv,
            middle,
            branch_one,
            own_tokens,
            modulation,
        )
        da_far = chip_swap(da_own)
        mrecv = chip_swap(after(msend, da_own))
        n_att = half + 16
        keep, send, att_keep, att_send = call(
            attention_back_kernel,
            [(shard, F32), (shard, BF16), ((2, 2, n_att, half), BF16), ((2, 2, n_att, half), BF16)],
            hidden_all,
            da_own,
            da_far,
            oqkv,
            soft,
            *att_weights,
            scalar=core_arg,
            flops=4 * LENGTH * width * 8 * cols,
            limit=58,
        )
        recv = chip_swap(send)
        if quick:
            att_core = core_swap(att_send)
            mlp_sum = total(mlp_sum[:, 0], after(mlp_rows, recv))
            recv = after(recv, mlp_sum)
            mlp_beside = col_swap(mlp_sum[1], 1)
        results, sums = call(
            last_kernel,
            [((2,) + shard, BF16), ((8, width), F32)],
            keep,
            recv,
            own_tokens,
            dmiddle,
            modulation,
            middle,
            mkeep,
            mrecv,
            sums_two,
        )

        ids = jnp.stack([labels, step_ids], axis=1).astype(F32)
        if quick:
            small = jnp.concatenate([cond_part, ids], axis=1)
            small = small.reshape(2, 2, 2, cond_cols + 2)
            small = at_odd(col_at % 2 == 1, small, 2)
            small = at_odd(col_at >= 2, small, 1)
            small = at_odd(row_at == 1, small, 0).reshape(2 * n_col, cond_cols + 2)
            small = jnp.concatenate([small, core_swap(after(small, middle))], axis=0)
            all_cond = small[:, :cond_cols]
            all_ids = small[:, cond_cols:]
            results = tokens_out(results)
            near = chip_swap(sums)
            att_sum = total(att_keep, after(att_core, near))
            att_rows = row_swap(att_sum[:, 1])
            sums = sums + near
            group = jnp.stack([sums, col_swap(sums, 1)])
            far = col_swap(group, 2)
            mlp_sum = total(mlp_sum[0], after(mlp_beside, far))
            mlp_last = lax.ppermute(mlp_sum, ALL, last_hop)
            att_sum = total(att_sum[:, 0], after(att_rows, far))
            far = after(far, mlp_sum, att_sum)
            att_beside = col_swap(att_sum[1], 1)
            group = jnp.stack([group, far]).reshape(n_col * 8, width)
            theirs = row_swap(group[:, half:])
            group = jnp.concatenate([group[:, :half], theirs], axis=0)
            other = core_swap(group)
            mlp_sum = total(mlp_sum, after(mlp_last, other))
            mlp_chip = to_chip(mlp_sum)
            other = after(other, mlp_sum, results)
            group = jnp.concatenate([group, other], axis=0)
            dmod = group.reshape(n_dp * n_col, 8, half)
        else:
            results = tokens_out(results)
            every = lax.all_gather(sums, ALL).reshape(2, 2, n_row // 2, 2, n_col, 8, width)
            every = jnp.sum(every, axis=0).transpose(2, 0, 3, 1, 4, 5)
            every = every.reshape(n_dp * sequences, 8, width)
            dmod = lax.dynamic_slice_in_dim(every, row_at * width_row, width_row, 2)
            all_cond = lax.all_gather(cond_part, "dp", axis=0, tiled=True)
            all_ids = lax.all_gather(ids, "dp", axis=0, tiled=True)

        gate = jax.nn.sigmoid(all_cond)
        all_act = all_cond * gate
        slope = gate * (1.0 + all_cond * (1.0 - gate))
        dmod_six = dmod[:, :6].reshape(-1, 6 * width_row)
        grad_ada = lax.dot_general(
            all_act, dmod_six, (((0,), (0,)), ((), ())), precision=PRECISE
        ).reshape(1, cond_cols, 6, width_row)
        totals = jnp.sum(dmod, axis=0)
        dact = jnp.sum(
            jnp.einsum("pbjf,djf->pbd", pieces_of(dmod[:, :6]), ada, preferred_element_type=F32), axis=0
        )
        if quick:
            flipped = row_swap(dact)
            flipped = flipped.reshape(2, 2, n_col, cond_cols)[:, ::-1]
            dcond = slope * (dact + flipped.reshape(-1, cond_cols))
            near = col_swap(dcond, 1)
            att_sum = total(att_sum[0], after(att_beside, near))
            att_last = lax.ppermute(att_sum, ALL, last_hop)
            near = near.reshape(-1, 2, cond_cols)[:, ::-1].reshape(dcond.shape)
            dcond = jnp.stack([dcond, near])
            far = col_swap(dcond, 2)
            far = far.reshape(-1, 2, 2, cond_cols)[:, ::-1]
            mlp_sum = jnp.where(at_source, mlp_sum, after(mlp_chip, far))
            mlp_core = core_swap(mlp_sum)
            att_sum = total(att_sum, after(att_last, far))
            att_chip = to_chip(att_sum)
            around = jnp.stack([dcond, far.reshape(dcond.shape)])
            around = at_odd(col_at % 2 == 1, around, 1)
            around = at_odd(col_at >= 2, around, 0)
            dcond = around.reshape(n_col, -1, cond_cols).transpose(1, 0, 2).reshape(-1, width)
        else:
            dcond = slope * lax.psum(dact, "row")
            dcond = lax.all_gather(dcond, "col", axis=1, tiled=True)
        all_ids = all_ids.astype(jnp.int32)
        grad_class = lax.dot_general(
            hot(all_ids[:, 0], class_rows).astype(F32), dcond, (((0,), (0,)), ((), ())), precision=PRECISE
        )
        grad_step = lax.dot_general(
            hot(all_ids[:, 1], step_rows).astype(F32), dcond, (((0,), (0,)), ((), ())), precision=PRECISE
        )

        def take(v, dim):
            return lax.dynamic_slice_in_dim(v, row_at * width_row, width_row, dim)

        def join(mine, theirs):
            return [
                jnp.where(core_at == 0, mine, theirs).astype(F32),
                jnp.where(core_at == 0, theirs, mine).astype(F32),
            ]

        def block_grads(att, mlp):
            qkv = jnp.concatenate([att[0][:half], att[1][:half, :cols]], axis=1)
            out = unfold(att[1][:half, cols:])
            up = jnp.concatenate([mlp[0][:half], mlp[1][:half]], axis=1)
            down = jnp.concatenate([mlp[0][half : 2 * half], mlp[1][half : 2 * half]], axis=0)
            bias_qkv = jnp.stack([att[0][half, :cols], att[1][half, :cols]])
            bias_up = jnp.stack([mlp[0][2 * half], mlp[1][2 * half]])
            return qkv, out, up, down, bias_qkv, bias_up

        if quick:
            att_sum = jnp.where(at_source, att_sum, att_chip)
            mlp_grads = join(mlp_sum, mlp_core)
            att_grads = join(att_sum, core_swap(att_sum))
            grad_qkv, grad_out, grad_up, grad_down, grad_bias_qkv, grad_bias_up = block_grads(
                att_grads, mlp_grads
            )
        else:

            def collect(keep, send):
                pieces = jnp.stack(join(keep, send))
                by_col = jnp.stack(
                    [
                        jnp.where(held_at == c, pieces[:, 0], 0.0) + jnp.where(beside_at == c, pieces[:, 1], 0.0)
                        for c in range(n_col)
                    ]
                )
                return lax.dynamic_index_in_dim(lax.psum(by_col, ALL), col_at, 0, keepdims=False)

            att = collect(att_keep, att_send)
            mlp = collect(mlp_keep, mlp_send)
            sides = [block_grads(att[:, side], mlp[:, side]) for side in (0, 1)]
            grad_qkv, grad_up = (
                take(jnp.concatenate([sides[0][at], sides[1][at]], axis=0), 0) for at in (0, 2)
            )
            grad_out, grad_down = (
                take(jnp.concatenate([sides[0][at], sides[1][at]], axis=1), 1) for at in (1, 3)
            )
            grad_bias_qkv, grad_bias_up = sides[0][4], sides[0][5]

        return (
            results[0],
            results[1],
            grad_class,
            grad_step,
            grad_ada,
            totals[None, :6],
            grad_qkv.reshape(1, width_row, 3, cols),
            grad_bias_qkv[None],
            grad_out[None],
            totals[None, 7],
            grad_up[None],
            grad_bias_up.reshape(1, hid),
            grad_down[None],
            totals[None, 6],
        )

    return body


def solution(mesh):
    return jax.shard_map(
        make_body(mesh.shape["dp"], mesh.shape["row"], mesh.shape["col"]),
        mesh=mesh,
        in_specs=(
            P(("dp", "col"), "row"),
            P("dp"),
            P("dp"),
            P("col", None),
            P("col", None),
            P(None, "col", None, "row"),
            P(None, None, "row"),
            P(None, "row", None, "col"),
            P(None, None, "col"),
            P(None, "col", "row"),
            P(None, "row"),
            P(None, "row", "col"),
            P(None, "col"),
            P(None, "col", "row"),
            P(None, "row"),
            P(("dp", "col"), "row"),
        ),
        out_specs=(
            P(("dp", "col"), "row"),
            P(("dp", "col"), "row"),
            P("col", None),
            P("col", None),
            P(None, "col", None, "row"),
            P(None, None, "row"),
            P(None, "row", None, "col"),
            P(None, None, "col"),
            P(None, "col", "row"),
            P(None, "row"),
            P(None, "row", "col"),
            P(None, "col"),
            P(None, "col", "row"),
            P(None, "row"),
        ),
        check_vma=False,
    )
```

```python
import jax
import jax.numpy as jnp
from jax import lax
from jax.experimental import pallas as pl
from jax.experimental.pallas import tpu as pltpu
from jax.sharding import PartitionSpec as P

HEAD_DIM = 64
LENGTH = 256
PRECISE = lax.Precision.HIGHEST
NORM_EPSILON = 1e-06
F32 = jnp.float32
BF16 = jnp.bfloat16
ALL = ("dp", "row", "col")
GELU_A = 0.7978845608028654
GELU_B = 0.044715


def dot(left, right):
    return lax.dot_general(left, right, (((1,), (0,)), ((), ())), preferred_element_type=F32)


def dot_t(left, right):
    return lax.dot_general(left, right, (((1,), (1,)), ((), ())), preferred_element_type=F32)


def t_dot(left, right):
    return lax.dot_general(left, right, (((0,), (0,)), ((), ())), preferred_element_type=F32)


def call(kernel, outs, *args, scalar=None, flops=0, limit=28):
    total = sum(a.size * a.dtype.itemsize for a in args)
    total += sum(s[0][-1] * s[0][-2] * 4 for s in outs)
    specs = [pl.BlockSpec(memory_space=pltpu.VMEM)] * len(args)
    if scalar is not None:
        specs = [pl.BlockSpec(memory_space=pltpu.SMEM)] + specs
        args = (scalar,) + args
    return pl.pallas_call(
        kernel,
        in_specs=specs,
        out_specs=[pl.BlockSpec(memory_space=pltpu.VMEM)] * len(outs),
        out_shape=[jax.ShapeDtypeStruct(shape, dtype) for shape, dtype in outs],
        compiler_params=pltpu.CompilerParams(vmem_limit_bytes=limit * 1024 * 1024),
        cost_estimate=pl.CostEstimate(flops=flops, bytes_accessed=total, transcendentals=0),
    )(*args)


def layer_norm(values):
    center = values - jnp.mean(values, axis=1, keepdims=True)
    inverse = lax.rsqrt(jnp.mean(center * center, axis=1, keepdims=True) + NORM_EPSILON)
    return center * inverse, inverse


def norm_back(grad, normed, inverse):
    return inverse * (
        grad
        - jnp.mean(grad, axis=1, keepdims=True)
        - normed * jnp.mean(grad * normed, axis=1, keepdims=True)
    )


def pick(index, values):
    chosen = jnp.int32(values[0])
    for at, value in enumerate(values[1:], 1):
        chosen = jnp.where(index == at, jnp.int32(value), chosen)
    return chosen


def after(value, *earlier):
    return lax.optimization_barrier((value,) + earlier)[0]


def pieces_of(values):
    high = lax.reduce_precision(values, 8, 7)
    rest = values - high
    middle = lax.reduce_precision(rest, 8, 7)
    return jnp.stack([high, middle, rest - middle]).astype(BF16)


def column_sum(values):
    return jnp.sum(values, axis=0, keepdims=True)


def unfold(folded):
    rows = folded.shape[0] // 2
    return jnp.concatenate([folded[:rows], folded[rows:]], axis=1)


def fold(values):
    lanes = values.shape[1] // 2
    return jnp.concatenate([values[:, :lanes], values[:, lanes:]], axis=0)


def by_core(core_ref, body, mine, theirs):
    @pl.when(core_ref[0] == 0)
    def _():
        body(0, mine, theirs)

    @pl.when(core_ref[0] == 1)
    def _():
        body(1, theirs, mine)


def attention_kernel(
    core_ref, tok_ref, mod_ref, a0, a1, a2, a3, b_ref,
    hid_ref, oqkv_ref, p_ref, keep_ref, send_ref,
):
    half = a0.shape[1]
    width = half // 2
    heads = width // HEAD_DIM
    normed, _ = layer_norm(jnp.concatenate([tok_ref[0], tok_ref[2]], axis=0).astype(F32))
    hidden = (normed * (1.0 + mod_ref[1:2, :]) + mod_ref[0:1, :]).astype(BF16)
    hid_ref[...] = hidden

    def body(_, first, second):
        total_m = total_o = None
        blocks = (
            (first[0], second[0], first[2], second[2]),
            (first[1], second[1], first[3], second[3]),
        )
        for which, (qk_m, vo_m, qk_o, vo_o) in enumerate(blocks):
            left, right = hidden[:, :half], hidden[:, half:]
            qk = dot(left, qk_m[:half, :]) + dot(right, qk_o[:half, :])
            qk = (qk + qk_m[half : half + 1, :].astype(F32)).astype(BF16)
            v = dot(left, vo_m[:half, :width]) + dot(right, vo_o[:half, :width])
            v = (v + vo_m[half : half + 1, :width].astype(F32)).astype(BF16)
            parts = []
            for head in range(heads):
                at = head * HEAD_DIM
                scores = dot_t(qk[:, at : at + HEAD_DIM], qk[:, width + at : width + at + HEAD_DIM])
                scores = scores * HEAD_DIM ** (-0.5)
                powers = jnp.exp(scores - jnp.max(scores, axis=1, keepdims=True))
                soft = powers * (1.0 / jnp.sum(powers, axis=1, keepdims=True))
                p_ref[which * heads + head] = soft
                parts.append(dot(soft.astype(BF16), v[:, at : at + HEAD_DIM]))
            attended = jnp.concatenate(parts, axis=1).astype(BF16)
            oqkv_ref[:, which * 2 * half : (which + 1) * 2 * half] = jnp.concatenate([attended, qk, v], axis=1)
            part_m = dot(attended, unfold(vo_m[:half, width:]))
            part_o = dot(attended, unfold(vo_o[:half, width:]))
            total_m = part_m if total_m is None else total_m + part_m
            total_o = part_o if total_o is None else total_o + part_o
        split(keep_ref, send_ref, total_m, total_o)

    by_core(core_ref, body, (a0, a1, a2, a3), [b_ref.at[at] for at in range(4)])


def split(keep_ref, send_ref, first, second):
    rows, half = first.shape[0] // 2, first.shape[1]
    keep_ref[:, :half] = first[:rows]
    keep_ref[:, half:] = second[:rows]
    send_ref[:, :half] = first[rows:].astype(BF16)
    send_ref[:, half:] = second[rows:].astype(BF16)


def second_norm_kernel(keep, recv, x_ref, mod_ref, a_ref, x1_ref, h_ref):
    branch = keep[...] + recv[...].astype(F32) + mod_ref[6:7, :]
    middle = x_ref[0].astype(F32) + mod_ref[2:3, :] * branch
    normed, _ = layer_norm(middle)
    a_ref[...] = branch
    x1_ref[...] = middle
    h_ref[...] = (normed * (1.0 + mod_ref[4:5, :]) + mod_ref[3:4, :]).astype(BF16)


def mlp_kernel(
    h0, h1, tok_ref, mod_ref, a0, a1, a2, a3, b_ref, b3,
    keep_ref, send_ref, mkeep, msend, gkeep, gsend,
):
    half = a0.shape[1]
    hidden = jnp.concatenate([h0[...], h1[...]], axis=0)
    dm = jnp.concatenate([tok_ref[1], tok_ref[3]], axis=0).astype(F32) * mod_ref[5:6, :]
    dm = dm.astype(BF16)
    left, right = hidden[:, :half], hidden[:, half:]
    dleft, dright = dm[:, :half], dm[:, half:]
    sums = None
    for own, oth, grads, which in (
        (a0, a2, gkeep, 0),
        (a1, a3, gkeep, 1),
        (b_ref.at[0], b_ref.at[1], gsend, 0),
        (b_ref.at[2], b3, gsend, 1),
    ):
        up = dot(left, own[:half, :]) + dot(right, oth[:half, :])
        up = up + own[2 * half : 2 * half + 1, :].astype(F32)
        square = up * up
        tanh = jnp.tanh(GELU_A * (up + GELU_B * up * square))
        act = (0.5 * up * (1.0 + tanh)).astype(BF16)
        slope = 0.5 * (1.0 + tanh) + 0.5 * up * (1.0 - tanh * tanh) * (
            GELU_A * (1.0 + 3.0 * GELU_B * square)
        )
        dg = dot_t(dleft, own[half : 2 * half, :]) + dot_t(dright, oth[half : 2 * half, :])
        du = (dg * slope).astype(BF16)
        parts = (
            dot_t(du, own[:half, :]),
            dot_t(du, oth[:half, :]),
            dot(act, own[half : 2 * half, :]),
            dot(act, oth[half : 2 * half, :]),
        )
        sums = parts if sums is None else tuple(a + b for a, b in zip(sums, parts))
        bias = jnp.pad(column_sum(du.astype(F32)), ((0, 15), (0, 0))).astype(BF16)
        for side, (tokens, dtokens) in enumerate(((left, dleft), (right, dright))):
            grads[which, side, :half, :] = t_dot(tokens, du).astype(BF16)
            grads[which, side, half : 2 * half, :] = t_dot(act, dtokens).astype(BF16)
            grads[which, side, 2 * half : 2 * half + 16, :] = bias
    split(keep_ref, send_ref, sums[0], sums[1])
    split(mkeep, msend, sums[2], sums[3])


def second_back_kernel(keep, recv, x1_ref, a_ref, tok_ref, mod_ref, da_ref, dx1_ref, sums_ref):
    dh = keep[...] + recv[...].astype(F32)
    normed, inverse = layer_norm(x1_ref[...])
    dy = tok_ref[1].astype(F32)
    dx1 = dy + norm_back(dh * (1.0 + mod_ref[4:5, :]), normed, inverse)
    da = (mod_ref[2:3, :] * dx1).astype(BF16)
    dx1_ref[...] = dx1
    da_ref[...] = da
    sums_ref[0:1, :] = column_sum(dx1 * a_ref[...])
    sums_ref[1:2, :] = column_sum(dh)
    sums_ref[2:3, :] = column_sum(dh * normed)
    sums_ref[3:4, :] = column_sum((mod_ref[5:6, :] * dy).astype(BF16).astype(F32))
    sums_ref[4:5, :] = column_sum(da.astype(F32))
    sums_ref[5:8, :] = jnp.zeros((3, sums_ref.shape[1]), F32)


def attention_back_kernel(
    core_ref, hid_ref, da0, da1, oqkv_ref, p_ref, a0, a1, a2, a3, b_ref,
    keep_ref, send_ref, gkeep, gsend,
):
    half = a0.shape[1]
    width = half // 2
    heads = width // HEAD_DIM
    scale = HEAD_DIM ** (-0.5)
    hidden = hid_ref[...]
    da = jnp.concatenate([da0[...], da1[...]], axis=0)
    da_sides = (da[:, :half], da[:, half:])
    h_sides = (hidden[:, :half], hidden[:, half:])

    def body(core, first, second):
        pieces = (gkeep, gsend) if core == 0 else (gsend, gkeep)
        total_m = total_o = None
        blocks = (
            (first[0], second[0], first[2], second[2]),
            (first[1], second[1], first[3], second[3]),
        )
        for which, (qk_m, vo_m, qk_o, vo_o) in enumerate(blocks):
            base = which * 2 * half
            attended = oqkv_ref[:, base : base + width]
            qk = oqkv_ref[:, base + width : base + 3 * width]
            values = oqkv_ref[:, base + 3 * width : base + 4 * width]
            do = dot_t(da_sides[0], unfold(vo_m[:half, width:]))
            do = (do + dot_t(da_sides[1], unfold(vo_o[:half, width:]))).astype(BF16)
            dqs, dks, dvs = [], [], []
            for head in range(heads):
                at = head * HEAD_DIM
                q = qk[:, at : at + HEAD_DIM]
                k = qk[:, width + at : width + at + HEAD_DIM]
                do_head = do[:, at : at + HEAD_DIM]
                soft = p_ref[which * heads + head]
                dsoft = dot_t(do_head, values[:, at : at + HEAD_DIM])
                ds = (soft * (dsoft - jnp.sum(soft * dsoft, axis=1, keepdims=True))).astype(BF16)
                dqs.append(dot(ds, k) * scale)
                dks.append(t_dot(ds, q) * scale)
                dvs.append(t_dot(soft.astype(BF16), do_head))
            dqk = jnp.concatenate(dqs + dks, axis=1).astype(BF16)
            dv = jnp.concatenate(dvs, axis=1).astype(BF16)
            part_m = dot_t(dqk, qk_m[:half, :]) + dot_t(dv, vo_m[:half, :width])
            part_o = dot_t(dqk, qk_o[:half, :]) + dot_t(dv, vo_o[:half, :width])
            total_m = part_m if total_m is None else total_m + part_m
            total_o = part_o if total_o is None else total_o + part_o
            bias_qk = jnp.pad(column_sum(dqk.astype(F32)), ((0, 15), (0, 0))).astype(BF16)
            bias_v = jnp.pad(column_sum(dv.astype(F32)), ((0, 15), (0, width))).astype(BF16)
            for side in (0, 1):
                pieces[0][which, side, :half, :] = t_dot(h_sides[side], dqk).astype(BF16)
                pieces[0][which, side, half : half + 16, :] = bias_qk
                grad_v = t_dot(h_sides[side], dv)
                grad_o = fold(t_dot(attended, da_sides[side]))
                pieces[1][which, side, :half, :] = jnp.concatenate([grad_v, grad_o], axis=1).astype(BF16)
                pieces[1][which, side, half : half + 16, :] = bias_v
        split(keep_ref, send_ref, total_m, total_o)

    by_core(core_ref, body, (a0, a1, a2, a3), [b_ref.at[at] for at in range(4)])


def last_kernel(
    keep, recv, tok_ref, dx1_ref, mod_ref, x1_ref, mkeep, mrecv, two_ref, out_ref, sums_ref
):
    dh = keep[...] + recv[...].astype(F32)
    normed, inverse = layer_norm(tok_ref[0].astype(F32))
    dx = dx1_ref[...] + norm_back(dh * (1.0 + mod_ref[1:2, :]), normed, inverse)
    branch = mkeep[...] + mrecv[...].astype(F32) + mod_ref[7:8, :]
    out_ref[0] = (x1_ref[...] + mod_ref[5:6, :] * branch).astype(BF16)
    out_ref[1] = dx.astype(BF16)
    sums_ref[0:1, :] = column_sum(dh)
    sums_ref[1:2, :] = column_sum(dh * normed)
    sums_ref[2:5, :] = two_ref[0:3, :]
    sums_ref[5:6, :] = column_sum(tok_ref[1].astype(F32) * branch)
    sums_ref[6:8, :] = two_ref[3:5, :]


def make_body(n_dp, n_row, n_col):
    def flat(d, r, c):
        return (d * n_row + r) * n_col + c

    places = [(d, r, c) for d in range(n_dp) for r in range(n_row) for c in range(n_col)]

    def core_swap(v):
        return lax.ppermute(v, "dp", [(d, d ^ 1) for d in range(n_dp)])

    def chip_swap(v):
        return lax.ppermute(v, "dp", [(d, d ^ 2) for d in range(n_dp)])

    def row_swap(v):
        return lax.ppermute(v, "row", [(0, 1), (1, 0)])

    def col_swap(v, bits):
        return lax.ppermute(v, "col", [(c, c ^ bits) for c in range(n_col)])

    def total(*parts):
        out = parts[0].astype(F32)
        for part in parts[1:]:
            out = out + part.astype(F32)
        return out.astype(BF16)

    def body(
        latents,
        labels,
        step_ids,
        class_table,
        step_table,
        w_ada,
        b_ada,
        w_qkv,
        b_qkv,
        w_out,
        b_out,
        w_up,
        b_up,
        w_down,
        b_down,
        cotangent,
    ):
        tokens, width_row = latents.shape
        per_block = tokens // LENGTH
        sequences = labels.shape[0]
        width = class_table.shape[1]
        half = width // 2
        cols = w_qkv.shape[3]
        hid = w_up.shape[2]
        cond_cols = w_ada.shape[1]
        quick = n_row == 2 and per_block == 1
        dp_at = lax.axis_index("dp")
        row_at = lax.axis_index("row")
        col_at = lax.axis_index("col")
        core_at = dp_at % 2
        near_at = dp_at // 2
        block = LENGTH // 2
        core_arg = core_at.astype(jnp.int32).reshape(1)

        owner = near_at == row_at % 2

        def at_odd(condition, v, axis):
            return jnp.where(condition, jnp.flip(v, axis), v)

        def gather_owner(own, other, *earlier):
            across = lax.ppermute(
                own, ALL, [(flat(d, r, c), flat(d, 1 - r, c)) for d, r, c in places if d // 2 != r]
            )
            across_near = lax.ppermute(
                other, ALL, [(flat(d, r, c), flat(d ^ 2, 1 - r, c)) for d, r, c in places if d // 2 != r]
            )
            near = lax.ppermute(
                other, ALL, [(flat(d, r, c), flat(d ^ 2, r, c)) for d, r, c in places if d // 2 == r]
            )
            across = after(across, *earlier)
            return jnp.concatenate(
                [jnp.where(owner, own, near), jnp.where(owner, across, across_near)], axis=-1
            )

        def tokens_in(v):
            if quick:
                own = lax.dynamic_slice_in_dim(v, near_at * block, block, 1)
                other = lax.dynamic_slice_in_dim(v, (1 - near_at) * block, block, 1)
                return gather_owner(
                    jnp.concatenate([own, other], axis=0), jnp.concatenate([other, own], axis=0)
                )
            full = lax.all_gather(v, "row", axis=2, tiled=True)
            full = jnp.where(owner, full, chip_swap(full))
            start = (row_at // 2) * LENGTH
            own = lax.dynamic_slice_in_dim(full, start + near_at * block, block, 1)
            other = lax.dynamic_slice_in_dim(full, start + (1 - near_at) * block, block, 1)
            return jnp.concatenate([own, other], axis=0)

        def tokens_out(v):
            if quick:
                mine, theirs = v[:, :, :half], v[:, :, half:]
                near = lax.ppermute(
                    mine, ALL, [(flat(d, r, c), flat(d ^ 2, r, c)) for d, r, c in places if d // 2 != r]
                )
                across = lax.ppermute(
                    theirs, ALL, [(flat(d, r, c), flat(d, 1 - r, c)) for d, r, c in places if d // 2 == r]
                )
                across_near = lax.ppermute(
                    theirs, ALL, [(flat(d, r, c), flat(d ^ 2, 1 - r, c)) for d, r, c in places if d // 2 != r]
                )
                first = jnp.where(owner, mine, across)
                second = jnp.where(owner, near, across_near)
                return jnp.where(
                    near_at == 0,
                    jnp.concatenate([first, second], axis=1),
                    jnp.concatenate([second, first], axis=1),
                )
            other = chip_swap(v)
            full = jnp.where(
                near_at == 0, jnp.concatenate([v, other], axis=1), jnp.concatenate([other, v], axis=1)
            )
            rows = lax.all_gather(full, "row", axis=1)
            rows = rows.reshape(2, n_row // 2, 2, LENGTH, width)
            rows = lax.dynamic_index_in_dim(rows, near_at, 2, keepdims=False)
            rows = rows.reshape(2, tokens, width)
            return lax.dynamic_slice_in_dim(rows, row_at * width_row, width_row, 2)

        first_hop = [
            (flat(d, r, a), flat(d, r, b))
            for d in range(n_dp)
            for r in range(n_row)
            for a, b in (((0, 2), (3, 1)) if d // 2 == 0 else ((1, 3), (2, 0)))
        ]
        last_hop = [(b, a) for a, b in first_hop]
        held_at = jnp.where(near_at == 0, pick(col_at, (0, 3, 0, 3)), pick(col_at, (2, 1, 2, 1)))
        beside_at = jnp.where(near_at == 0, pick(col_at, (3, 0, 3, 0)), pick(col_at, (1, 2, 1, 2)))
        at_source = held_at == col_at

        def pack_attention(w, out):
            bias = jnp.concatenate(
                [b_qkv[0, 0], jnp.zeros((cols,), BF16), b_qkv[0, 1], jnp.zeros((cols,), BF16)]
            ).reshape(2, 1, 2 * cols)
            bias = jnp.pad(bias, ((0, 0), (0, 15), (0, 0)))
            second = jnp.concatenate([w[:, 2 * cols :], fold(out)], axis=1)
            return jnp.concatenate([jnp.stack([w[:, : 2 * cols], second]), bias], axis=1)

        def pack_mlp(up, down):
            bias = jnp.pad(b_up.reshape(2, 1, half), ((0, 0), (0, 15), (0, 0)))
            return jnp.concatenate(
                [jnp.stack([up[:, :half], up[:, half:]]), down.reshape(2, half, half), bias], axis=1
            )

        def by_piece(v):
            return jnp.where(core_at == 0, v[0], v[1]), jnp.where(core_at == 0, v[1], v[0])

        if quick:
            own_att = pack_attention(w_qkv[0].reshape(width_row, 3 * cols), w_out[0])
            piece = by_piece(own_att)[0]
            own_ids = jnp.stack([labels, step_ids], axis=1)
            other = chip_swap(own_ids)
            chips = jnp.where(near_at == 0, jnp.stack([own_ids, other]), jnp.stack([other, own_ids]))
            labels, step_ids = chips[:, :, 0].reshape(-1), chips[:, :, 1].reshape(-1)
            mlp_piece = by_piece(after(pack_mlp(w_up[0], w_down[0]), piece))[0]

        def to_chip(v):
            return lax.ppermute(
                v,
                ALL,
                [(flat(d, r, c), flat(d ^ 2, r, c)) for d, r, c in places if (d // 2 == 0) == (c in (0, 3))],
            )

        class_rows = class_table.shape[0]
        step_rows = step_table.shape[0]

        def hot(ids, rows):
            return ids[:, None] == (col_at * rows + jnp.arange(rows, dtype=jnp.int32))[None, :]

        partial_cond = dot(hot(labels, class_rows).astype(BF16), class_table) + dot(
            hot(step_ids, step_rows).astype(BF16), step_table
        )
        ada = w_ada[0]
        small_bias = jnp.concatenate([b_ada[0], b_out, b_down], axis=0).astype(F32)
        if quick:
            near = col_swap(partial_cond, 1)
            condition = (partial_cond + near) + (
                col_swap(partial_cond, 2) + col_swap(partial_cond, 3)
            )
        else:
            condition = lax.psum(partial_cond, "col")
        cond_part = lax.dynamic_slice_in_dim(condition, col_at * cond_cols, cond_cols, 1)
        act_part = cond_part * jax.nn.sigmoid(cond_part)
        if quick:
            own_tokens = tokens_in(after(jnp.stack([latents, cotangent]), condition))
            att_first = lax.ppermute(after(piece, condition), ALL, first_hop)
            held = jnp.where(at_source, piece, att_first)
            beside = col_swap(held, 1)
        mod_part = jnp.sum(
            jnp.einsum("pbd,djf->pbjf", pieces_of(act_part), ada, preferred_element_type=F32), axis=0
        ).reshape(act_part.shape[0], -1)
        if quick:
            turned = at_odd(col_at % 2 == 1, mod_part.reshape(2, 2, 2, -1), 2)
            turned = at_odd(col_at >= 2, turned, 1).reshape(2, n_col, -1)
            mod_sum = (turned[:, 0] + col_swap(turned[:, 1], 1)) + (
                col_swap(turned[:, 2], 2) + col_swap(turned[:, 3], 3)
            )
            mod_sum = after(mod_sum, held, own_tokens)
            both = jnp.concatenate([mod_sum.reshape(2, 6, width_row), jnp.zeros((2, 2, width_row), F32)], axis=1)
            both = both + small_bias[None]
            both = at_odd(row_at == 1, both, 0)
            other = row_swap(both[1])
            held_row = row_swap(after(held, other))
            beside_row = row_swap(after(beside, other))
            modulation = jnp.concatenate([both[0], other], axis=1)
        else:
            all_mod = lax.psum(mod_part, "col").reshape(sequences, 6, width_row)
            all_mod = jnp.concatenate([all_mod, jnp.zeros((sequences, 2, width_row), F32)], axis=1)
            all_mod = lax.all_gather(all_mod + small_bias[None], "row", axis=2, tiled=True)
            all_mod = jnp.where(owner, all_mod, chip_swap(all_mod))
            modulation = lax.dynamic_index_in_dim(
                all_mod, col_at * per_block + row_at // 2, 0, keepdims=False
            )

        def from_partner(mine):
            return core_swap(jnp.stack(mine))

        if quick:
            att_mine = (held, beside, held_row, beside_row)
            mlp_first = lax.ppermute(after(mlp_piece, beside), ALL, first_hop)
            held = jnp.where(at_source, mlp_piece, mlp_first)
            att_theirs = from_partner(att_mine[:3] + (after(att_mine[3], held),))
            beside = col_swap(held, 1)
            held_row = row_swap(held)
            own_tokens = after(own_tokens, beside, held_row)
            beside_row = row_swap(beside)
        else:
            own_tokens = tokens_in(jnp.stack([latents, cotangent]))
            full_qkv = lax.all_gather(w_qkv[0].reshape(width_row, 3 * cols), "row", axis=0, tiled=True)
            full_out = lax.all_gather(w_out[0], "row", axis=1, tiled=True)
            full_up = lax.all_gather(w_up[0], "row", axis=0, tiled=True)
            full_down = lax.all_gather(w_down[0], "row", axis=1, tiled=True)

            def fetch(first, second):
                every = lax.all_gather(jnp.stack([first, second]), "col")
                parts = [
                    by_piece(lax.dynamic_index_in_dim(every, at, 0, keepdims=False)[side])
                    for side in (0, 1)
                    for at in (held_at, beside_at)
                ]
                return tuple(v[0] for v in parts), jnp.stack([v[1] for v in parts])

            att_mine, att_theirs = fetch(
                pack_attention(full_qkv[:half], full_out[:, :half]),
                pack_attention(full_qkv[half:], full_out[:, half:]),
            )
            mlp_mine, mlp_theirs = fetch(
                pack_mlp(full_up[:half], full_down[:, :half]), pack_mlp(full_up[half:], full_down[:, half:])
            )
            mlp_theirs = mlp_theirs[jnp.array([0, 2, 1])], mlp_theirs[3]
        att_weights = att_mine + (att_theirs,)

        heads = 2 * cols // HEAD_DIM
        shard = (block, width)
        hidden_all, oqkv, soft, keep, send = call(
            attention_kernel,
            [
                ((LENGTH, width), BF16),
                ((LENGTH, 8 * cols), BF16),
                ((heads, LENGTH, LENGTH), F32),
                (shard, F32),
                (shard, BF16),
            ],
            own_tokens,
            modulation,
            *att_weights,
            scalar=core_arg,
            flops=2 * LENGTH * width * 8 * cols,
        )
        recv = chip_swap(send)
        branch_one, middle, hm_own = call(
            second_norm_kernel,
            [(shard, F32), (shard, F32), (shard, BF16)],
            keep,
            recv,
            own_tokens,
            modulation,
        )

        hm_far = chip_swap(hm_own)
        if quick:
            beside_row = after(beside_row, hm_far)
            mlp_mine = (held, beside, held_row, beside_row)
            mlp_theirs = from_partner((held, held_row, beside)), core_swap(beside_row)

        n_mlp = 2 * half + 16
        grads = ((2, 2, n_mlp, half), BF16)
        keep, send, mkeep, msend, mlp_keep, mlp_send = call(
            mlp_kernel,
            [(shard, F32), (shard, BF16), (shard, F32), (shard, BF16), grads, grads],
            hm_own,
            hm_far,
            own_tokens,
            modulation,
            *mlp_mine,
            *mlp_theirs,
            flops=24 * LENGTH * width * hid,
        )
        recv = chip_swap(send)
        if quick:
            mlp_sum = total(mlp_keep, after(core_swap(mlp_send), recv))
            recv = after(recv, mlp_sum)
            mlp_rows = row_swap(mlp_sum[:, 1])
        da_own, dmiddle, sums_two = call(
            second_back_kernel,
            [(shard, BF16), (shard, F32), ((8, width), F32)],
            keep,
            recv,
            middle,
            branch_one,
            own_tokens,
            modulation,
        )
        da_far = chip_swap(da_own)
        mrecv = chip_swap(after(msend, da_own))
        n_att = half + 16
        keep, send, att_keep, att_send = call(
            attention_back_kernel,
            [(shard, F32), (shard, BF16), ((2, 2, n_att, half), BF16), ((2, 2, n_att, half), BF16)],
            hidden_all,
            da_own,
            da_far,
            oqkv,
            soft,
            *att_weights,
            scalar=core_arg,
            flops=4 * LENGTH * width * 8 * cols,
            limit=58,
        )
        recv = chip_swap(send)
        if quick:
            att_core = core_swap(att_send)
            mlp_sum = total(mlp_sum[:, 0], after(mlp_rows, recv))
            mlp_beside = col_swap(mlp_sum[1], 1)
        results, sums = call(
            last_kernel,
            [((2,) + shard, BF16), ((8, width), F32)],
            keep,
            recv,
            own_tokens,
            dmiddle,
            modulation,
            middle,
            mkeep,
            mrecv,
            sums_two,
        )

        ids = jnp.stack([labels, step_ids], axis=1).astype(F32)
        if quick:
            small = jnp.concatenate([cond_part, ids], axis=1)
            small = small.reshape(2, 2, 2, cond_cols + 2)
            small = at_odd(col_at % 2 == 1, small, 2)
            small = at_odd(col_at >= 2, small, 1)
            small = at_odd(row_at == 1, small, 0).reshape(2 * n_col, cond_cols + 2)
            small = jnp.concatenate([small, core_swap(after(small, middle))], axis=0)
            all_cond = small[:, :cond_cols]
            all_ids = small[:, cond_cols:]
            results = tokens_out(results)
            near = chip_swap(sums)
            att_sum = total(att_keep, after(att_core, near))
            att_rows = row_swap(att_sum[:, 1])
            sums = sums + near
            group = jnp.stack([sums, col_swap(sums, 1)])
            far = col_swap(group, 2)
            mlp_sum = total(mlp_sum[0], after(mlp_beside, far))
            mlp_last = lax.ppermute(mlp_sum, ALL, last_hop)
            att_sum = total(att_sum[:, 0], after(att_rows, far))
            far = after(far, mlp_sum, att_sum)
            att_beside = col_swap(att_sum[1], 1)
            group = jnp.stack([group, far]).reshape(n_col * 8, width)
            theirs = row_swap(group[:, half:])
            group = jnp.concatenate([group[:, :half], theirs], axis=0)
            other = core_swap(group)
            mlp_sum = total(mlp_sum, after(mlp_last, other))
            mlp_chip = to_chip(mlp_sum)
            other = after(other, mlp_sum, results)
            group = jnp.concatenate([group, other], axis=0)
            dmod = group.reshape(n_dp * n_col, 8, half)
        else:
            results = tokens_out(results)
            every = lax.all_gather(sums, ALL).reshape(2, 2, n_row // 2, 2, n_col, 8, width)
            every = jnp.sum(every, axis=0).transpose(2, 0, 3, 1, 4, 5)
            every = every.reshape(n_dp * sequences, 8, width)
            dmod = lax.dynamic_slice_in_dim(every, row_at * width_row, width_row, 2)
            all_cond = lax.all_gather(cond_part, "dp", axis=0, tiled=True)
            all_ids = lax.all_gather(ids, "dp", axis=0, tiled=True)

        gate = jax.nn.sigmoid(all_cond)
        all_act = all_cond * gate
        slope = gate * (1.0 + all_cond * (1.0 - gate))
        dmod_six = dmod[:, :6].reshape(-1, 6 * width_row)
        grad_ada = lax.dot_general(
            all_act, dmod_six, (((0,), (0,)), ((), ())), precision=PRECISE
        ).reshape(1, cond_cols, 6, width_row)
        totals = jnp.sum(dmod, axis=0)
        dact = jnp.sum(
            jnp.einsum("pbjf,djf->pbd", pieces_of(dmod[:, :6]), ada, preferred_element_type=F32), axis=0
        )
        if quick:
            flipped = row_swap(dact)
            flipped = flipped.reshape(2, 2, n_col, cond_cols)[:, ::-1]
            dcond = slope * (dact + flipped.reshape(-1, cond_cols))
            near = col_swap(dcond, 1)
            att_sum = total(att_sum[0], after(att_beside, near))
            att_last = lax.ppermute(att_sum, ALL, last_hop)
            near = near.reshape(-1, 2, cond_cols)[:, ::-1].reshape(dcond.shape)
            dcond = jnp.stack([dcond, near])
            far = col_swap(dcond, 2)
            far = far.reshape(-1, 2, 2, cond_cols)[:, ::-1]
            mlp_sum = jnp.where(at_source, mlp_sum, after(mlp_chip, far))
            mlp_core = core_swap(mlp_sum)
            att_sum = total(att_sum, after(att_last, far))
            att_chip = to_chip(att_sum)
            around = jnp.stack([dcond, far.reshape(dcond.shape)])
            around = at_odd(col_at % 2 == 1, around, 1)
            around = at_odd(col_at >= 2, around, 0)
            dcond = around.reshape(n_col, -1, cond_cols).transpose(1, 0, 2).reshape(-1, width)
        else:
            dcond = slope * lax.psum(dact, "row")
            dcond = lax.all_gather(dcond, "col", axis=1, tiled=True)
        all_ids = all_ids.astype(jnp.int32)
        grad_class = lax.dot_general(
            hot(all_ids[:, 0], class_rows).astype(F32), dcond, (((0,), (0,)), ((), ())), precision=PRECISE
        )
        grad_step = lax.dot_general(
            hot(all_ids[:, 1], step_rows).astype(F32), dcond, (((0,), (0,)), ((), ())), precision=PRECISE
        )

        def take(v, dim):
            return lax.dynamic_slice_in_dim(v, row_at * width_row, width_row, dim)

        def join(mine, theirs):
            return [
                jnp.where(core_at == 0, mine, theirs).astype(F32),
                jnp.where(core_at == 0, theirs, mine).astype(F32),
            ]

        def block_grads(att, mlp):
            if att is None:
                up = jnp.concatenate([mlp[0][:half], mlp[1][:half]], axis=1)
                down = jnp.concatenate([mlp[0][half : 2 * half], mlp[1][half : 2 * half]], axis=0)
                return up, down, jnp.stack([mlp[0][2 * half], mlp[1][2 * half]])
            qkv = jnp.concatenate([att[0][:half], att[1][:half, :cols]], axis=1)
            out = unfold(att[1][:half, cols:])
            return qkv, out, jnp.stack([att[0][half, :cols], att[1][half, :cols]])

        if quick:
            mlp_grads = join(mlp_sum, mlp_core)
            mlp_grads = block_grads(None, mlp_grads)
            grad_up, grad_down, grad_bias_up = mlp_grads
            att_sum = jnp.where(at_source, att_sum, after(att_chip, grad_up, grad_down))
            att_grads = join(att_sum, core_swap(att_sum))
            grad_qkv, grad_out, grad_bias_qkv = block_grads(att_grads, None)
        else:

            def collect(keep, send):
                pieces = jnp.stack(join(keep, send))
                by_col = jnp.stack(
                    [
                        jnp.where(held_at == c, pieces[:, 0], 0.0) + jnp.where(beside_at == c, pieces[:, 1], 0.0)
                        for c in range(n_col)
                    ]
                )
                return lax.dynamic_index_in_dim(lax.psum(by_col, ALL), col_at, 0, keepdims=False)

            att = collect(att_keep, att_send)
            mlp = collect(mlp_keep, mlp_send)
            sides = []
            for side in (0, 1):
                qkv_part, out_part, bias_part = block_grads(att[:, side], None)
                up_part, down_part, up_bias = block_grads(None, mlp[:, side])
                sides.append((qkv_part, out_part, up_part, down_part, bias_part, up_bias))
            grad_qkv, grad_up = (
                take(jnp.concatenate([sides[0][at], sides[1][at]], axis=0), 0) for at in (0, 2)
            )
            grad_out, grad_down = (
                take(jnp.concatenate([sides[0][at], sides[1][at]], axis=1), 1) for at in (1, 3)
            )
            grad_bias_qkv, grad_bias_up = sides[0][4], sides[0][5]

        return (
            results[0],
            results[1],
            grad_class,
            grad_step,
            grad_ada,
            totals[None, :6],
            grad_qkv.reshape(1, width_row, 3, cols),
            grad_bias_qkv[None],
            grad_out[None],
            totals[None, 7],
            grad_up[None],
            grad_bias_up.reshape(1, hid),
            grad_down[None],
            totals[None, 6],
        )

    return body


def solution(mesh):
    return jax.shard_map(
        make_body(mesh.shape["dp"], mesh.shape["row"], mesh.shape["col"]),
        mesh=mesh,
        in_specs=(
            P(("dp", "col"), "row"),
            P("dp"),
            P("dp"),
            P("col", None),
            P("col", None),
            P(None, "col", None, "row"),
            P(None, None, "row"),
            P(None, "row", None, "col"),
            P(None, None, "col"),
            P(None, "col", "row"),
            P(None, "row"),
            P(None, "row", "col"),
            P(None, "col"),
            P(None, "col", "row"),
            P(None, "row"),
            P(("dp", "col"), "row"),
        ),
        out_specs=(
            P(("dp", "col"), "row"),
            P(("dp", "col"), "row"),
            P("col", None),
            P("col", None),
            P(None, "col", None, "row"),
            P(None, None, "row"),
            P(None, "row", None, "col"),
            P(None, None, "col"),
            P(None, "col", "row"),
            P(None, "row"),
            P(None, "row", "col"),
            P(None, "col"),
            P(None, "col", "row"),
            P(None, "row"),
        ),
        check_vma=False,
    )
```
